32 devices in a mesh: bucket: 4 (over x, core), edge: 8 (over z, y).
Axes of the slice: x: 2, y: 2, z: 4, core: 2. Of those that a mesh axis runs over, the one named last changes fastest.
Arguments:
- left_emb: float32 [8192, 400], P(('bucket', 'edge')), may hold values from -20 to 20
- right_emb: float32 [8192, 400], P(('bucket', 'edge')), may hold values from -20 to 20
- left_state: float32 [8192], P(('bucket', 'edge')), may hold values from 0.1 to 10
- right_state: float32 [8192], P(('bucket', 'edge')), may hold values from 0.1 to 10
- relations: float32 [1024, 400], replicated, may hold values from 0.1 to 1.9
- src_rows: int32 [4, 2, 2048], P('bucket', None, 'edge'), may hold values from 0 to 2047, as said below
- dst_rows: int32 [4, 2, 2048], P('bucket', None, 'edge'), may hold values from 0 to 2047, as said below
- rel_ids: int32 [4, 2, 2048], P('bucket', None, 'edge'), may hold values from 0 to 1023
- neg_rows: int32 [4, 2, 2048], P('bucket', None, 'edge'), may hold values from 0 to 2047, as said below
Outputs:
- left_next: float32 [8192, 400], P(('bucket', 'edge'))
- left_state_next: float32 [8192], P(('bucket', 'edge'))
- right_next: float32 [8192, 400], P(('bucket', 'edge'))
- right_state_next: float32 [8192], P(('bucket', 'edge'))
The draws below stay inside these ranges and needn't reach their ends.
Inputs may be any that keep to these rules, and one draw needn't show every extreme that they name: `src_rows`: of the 256 sources of one bucket, sub-round and index of edge, at most 36 lie in the rows held by any one index of edge; in each bucket and sub-round one index's rows receive exactly 36 from every index. `dst_rows`: likewise for the 256 destinations of one bucket, sub-round and index of edge. `neg_rows`: likewise for the 256 negatives of one bucket, sub-round and index of edge; a block's negatives may repeat rows and may equal its edges' destinations.
All inputs are finite; a program needn't handle non-finite values.
Results may differ from the reference program's by a relative error of at most 0.0037.
Values may be sent and summed in bfloat16 or wider, within the bound.
A program may use at most 64 MiB of HBM per device.

```python
import math
import jax
import jax.numpy as jnp
from jax import lax

D = 400
CH = 256
NEG = 256
SUBS = 2
REL = 1024
R_DEV = 256
ROWS = 2048
BUCKETS = 4
EDGES = 2048
N_BUCKET = 4
N_EDGE = 8


def embed_rows(key, lower, upper):
    first = jax.random.fold_in(key, 0)
    fourth = jax.random.fold_in(key, 3)
    shape = (BUCKETS * ROWS, D)
    rough = jnp.clip(jax.random.normal(first, shape, jnp.float32), -6.0, 6.0)
    scale = jnp.exp(jax.random.uniform(fourth, (BUCKETS * ROWS, 1), jnp.float32, math.log(lower), math.log(upper)))
    return scale * rough


def draw_left_emb(key, part):
    key = jax.random.fold_in(key, 11)
    return embed_rows(key, 0.3, 3.0)


def draw_right_emb(key, part):
    key = jax.random.fold_in(key, 23)
    return embed_rows(key, 0.3, 3.0)


def routed_rows(key, count):
    holders = ROWS // R_DEV
    slot_cap = max(CH, NEG) // holders + 4
    slot_total = holders * slot_cap

    def one_list(list_key, full):
        first, second, third = jax.random.split(list_key, 3)
        score = jax.random.permutation(first, slot_total).astype(jnp.int32)
        owner_of = jnp.arange(slot_total, dtype=jnp.int32) // slot_cap
        score = score + jnp.where(owner_of == full, slot_total, 0).astype(jnp.int32)
        picked = jnp.argsort(-score, stable=True)[:count].astype(jnp.int32)
        picked = jax.random.permutation(second, picked)
        offset = jax.random.randint(third, (count,), 0, R_DEV, jnp.int32)
        return picked // slot_cap * R_DEV + offset

    def one_group(group_key):
        full = jax.random.randint(jax.random.fold_in(group_key, 0), (), 0, holders, jnp.int32)
        list_keys = jax.random.split(jax.random.fold_in(group_key, 1), holders)
        return jax.vmap(lambda sub_key: one_list(sub_key, full))(list_keys)
    group_keys = jax.random.split(key, BUCKETS * SUBS)
    lists = jax.vmap(one_group)(group_keys)
    return lists.reshape(BUCKETS, SUBS, holders * count).astype(jnp.int32)


def draw_src_rows(key, part):
    key = jax.random.fold_in(key, 31)
    return routed_rows(key, CH)


def draw_dst_rows(key, part):
    key = jax.random.fold_in(key, 37)
    return routed_rows(key, CH)


def draw_neg_rows(key, part):
    key = jax.random.fold_in(key, 41)
    return routed_rows(key, NEG)


def touch_ends(values, key, least, top_value):
    longest = values.shape.index(max(values.shape))
    spots = []
    for shift in (0, 1):
        where = [jax.random.randint(jax.random.fold_in(key, axis), (), 0, length) for axis, length in enumerate(values.shape)]
        where[longest] = (where[longest] + shift) % values.shape[longest]
        spots.append(tuple(where))
    return values.at[spots[0]].set(least).at[spots[1]].set(top_value)


def block_scale(key, shape, cuts, smallest, top_value):
    level = 1.0
    for position, parts in cuts:
        heights = jax.random.uniform(jax.random.fold_in(jax.random.fold_in(key, 6), position), (parts,), jnp.float32, smallest / len(cuts), top_value / len(cuts))
        level = level * jnp.repeat(jnp.exp(heights), shape[position] // parts).reshape((-1,) + (1,) * (len(shape) - 1 - position))
    return level


def setup_inputs(seed: int = 0) -> dict:
    keys = jax.random.split(jax.random.key(seed), 10)
    left_emb = draw_left_emb(jax.random.fold_in(keys[9], 71), 0)
    right_emb = draw_right_emb(jax.random.fold_in(keys[9], 71), 0)
    left_state = jnp.clip(jnp.exp(math.log(10.0) - 4.6051702 * jax.random.uniform(keys[2], (BUCKETS * ROWS,), jnp.float32) ** block_scale(keys[2], (BUCKETS * ROWS,), ((0, 32),), -0.2, 0.2)), 0.1, 10.0)
    right_state = jnp.clip(jnp.exp(math.log(10.0) - 4.6051702 * jax.random.uniform(keys[3], (BUCKETS * ROWS,), jnp.float32) ** block_scale(keys[3], (BUCKETS * ROWS,), ((0, 32),), -0.2, 0.2)), 0.1, 10.0)
    relations = jnp.clip(1.0 + 0.18 * jax.random.normal(keys[4], (REL, D), jnp.float32), 0.1, 1.9)
    src_rows = draw_src_rows(jax.random.fold_in(keys[9], 71), 0)
    dst_rows = draw_dst_rows(jax.random.fold_in(keys[9], 71), 0)
    rel_ids = touch_ends(jax.random.randint(keys[7], (BUCKETS, SUBS, EDGES), 0, REL), jax.random.fold_in(keys[7], 1), 0, REL - 1).astype(jnp.int32)
    neg_rows = draw_neg_rows(jax.random.fold_in(keys[9], 71), 0)
    return {"left_emb": left_emb, "right_emb": right_emb, "left_state": left_state, "right_state": right_state, "relations": relations, "src_rows": src_rows, "dst_rows": dst_rows, "rel_ids": rel_ids, "neg_rows": neg_rows}


sharp = 40.0
rate = 0.5
tiny = 1e-06
guard = 1e-10

def unit(vectors):
    length = jnp.sqrt(lax.optimization_barrier(jnp.sum(vectors * vectors, axis=-1, keepdims=True)) + tiny)
    return (vectors / length, length)

def unit_back(grad, direction, length):
    return (grad - direction * lax.optimization_barrier(jnp.sum(direction * grad, axis=-1, keepdims=True))) / length

def contract(first, second, dims):
    return lax.dot_general(first, second, (dims, ((), ())), preferred_element_type=jnp.float32)

def block_grads(left_copy, right_copy, relations, sources, targets, kinds, noises):
    scale = relations[kinds]
    query, query_len = unit(left_copy[sources].astype(jnp.float32) * scale)
    target, target_len = unit(right_copy[targets].astype(jnp.float32))
    noise, noise_len = unit(right_copy[noises].astype(jnp.float32))
    query_half = query.astype(jnp.bfloat16)
    noise_half = noise.astype(jnp.bfloat16)
    positive = sharp * lax.optimization_barrier(jnp.sum(query * target, axis=1))
    scores = sharp * contract(query_half, noise_half, ((1,), (1,)))
    raised = jnp.exp(positive)
    spread = jnp.exp(scores)
    total = raised + lax.optimization_barrier(jnp.sum(spread, axis=1))
    miss = raised / total - 1.0
    weights = (spread / total[:, None]).astype(jnp.bfloat16)
    query_grad = sharp * (miss[:, None] * target + contract(weights, noise_half, ((1,), (0,))))
    target_grad = sharp * miss[:, None] * query
    noise_grad = sharp * contract(weights, query_half, ((0,), (0,)))
    return (unit_back(query_grad, query, query_len) * scale, unit_back(target_grad, target, target_len), unit_back(noise_grad, noise, noise_len))

def adagrad(matrix, state, grad):
    state = state + lax.optimization_barrier(jnp.mean(grad * grad, axis=1))
    return (matrix - rate * grad / (jnp.sqrt(state)[:, None] + guard), state)

def reference(left_emb, right_emb, left_state, right_state, relations, src_rows, dst_rows, rel_ids, neg_rows):
    left = left_emb.reshape(N_BUCKET, ROWS, D)
    right = right_emb.reshape(N_BUCKET, ROWS, D)
    left_acc = left_state.reshape(N_BUCKET, ROWS)
    right_acc = right_state.reshape(N_BUCKET, ROWS)
    for step in range(SUBS):

        def bucket(items):
            left_part, right_part, left_hist, right_hist, sources, targets, kinds, noises = items
            left_copy = left_part.astype(jnp.bfloat16)
            right_copy = right_part.astype(jnp.bfloat16)

            def block(carry, pieces):
                left_grad, right_grad = carry
                source, target, kind, noise = pieces
                grads = block_grads(left_copy, right_copy, relations, source, target, kind, noise)
                left_grad = left_grad + jax.ops.segment_sum(grads[0], source, num_segments=ROWS)
                right_grad = right_grad + jax.ops.segment_sum(grads[1], target, num_segments=ROWS)
                right_grad = right_grad + jax.ops.segment_sum(grads[2], noise, num_segments=ROWS)
                return ((left_grad, right_grad), None)
            zeros = jnp.zeros((ROWS, D), jnp.float32)
            (left_grad, right_grad), unused = lax.scan(block, (zeros, zeros), (sources.reshape(N_EDGE, CH), targets.reshape(N_EDGE, CH), kinds.reshape(N_EDGE, CH), noises.reshape(N_EDGE, NEG)))
            left_new, left_hist = adagrad(left_part, left_hist, left_grad)
            right_new, right_hist = adagrad(right_part, right_hist, right_grad)
            return (left_new, right_new, left_hist, right_hist)
        left, right, left_acc, right_acc = lax.map(bucket, (left, right, left_acc, right_acc, src_rows[:, step], dst_rows[:, step], rel_ids[:, step], neg_rows[:, step]))
    right = jnp.roll(right, 1, axis=0)
    right_acc = jnp.roll(right_acc, 1, axis=0)
    return (left.reshape(N_BUCKET * ROWS, D), left_acc.reshape(N_BUCKET * ROWS), right.reshape(N_BUCKET * ROWS, D), right_acc.reshape(N_BUCKET * ROWS))
```

```python
import functools

import jax
import jax.numpy as jnp
from jax import lax
from jax.experimental import pallas as pl
from jax.experimental.pallas import tpu as pltpu
from jax.sharding import PartitionSpec as P

SUBS = 2
LANE = 128
PACK = 16

sharp = 40.0
rate = 0.5
tiny = 1e-06
guard = 1e-10

f32 = jnp.float32
bf16 = jnp.bfloat16
MESH = pl.DeviceIdType.MESH


def dot(first, second, dims=((1,), (0,))):
    return lax.dot_general(first, second, (dims, ((), ())), preferred_element_type=f32)


def iota(shape, dim):
    return lax.broadcasted_iota(jnp.int32, shape, dim)


def to_column(row):
    n = row.shape[1]
    same = iota((n, n), 0) == iota((n, n), 1)
    return jnp.sum(jnp.where(same, row, 0.0), axis=1, keepdims=True)


def to_row(column):
    n = column.shape[0]
    same = iota((n, n), 0) == iota((n, n), 1)
    return jnp.sum(jnp.where(same, column, 0.0), axis=0, keepdims=True)


def one_hot(where):
    return jnp.where(where, 1.0, 0.0).astype(bf16)


def kernel(
    n, nb, width, cap, slots,
    left_ref, right_ref, lstate_ref, rstate_ref, rel_hbm, src_ref, dst_ref, kind_ref, neg_ref,
    lout_ref, lsout_ref, rout_ref, rsout_ref,
    lbuf, rbuf, lcol, rcol, table, rel_raw, rel_hi, rel_lo, scale,
    place, place_t, pick, pick_t, prow, lrow, flat, fetched, grads,
    wsend, wrecv, msend, mrecv, ssend, srecv,
    wsem_s, wsem_r, msem_s, msem_r, ssem, rel_sem,
):
    rows = left_ref.shape[0]
    edges = src_ref.shape[1]
    wide = lbuf.shape[1]
    main = wide - LANE
    tail = width - main
    groups = slots // PACK
    chunks = main // LANE
    me = lax.axis_index("edge")
    mb = lax.axis_index("bucket")
    after = lax.rem(mb + 1, nb)
    before = lax.rem(mb + nb - 1, nb)

    def partner(j):
        return lax.rem(me + n // 2 + ((j + 1) // 2) * (2 * (j % 2) - 1) + n, n)

    def each_partner(body):
        def step(j, carry):
            body(partner(j))
            return carry
        lax.fori_loop(0, n - 1, step, 0)

    def each_index(body):
        def step(j, carry):
            body(j)
            return carry
        lax.fori_loop(0, n, step, 0)

    barrier = pltpu.get_barrier_semaphore()

    def greet(p):
        pl.semaphore_signal(barrier, inc=1, device_id=(mb, p), device_id_type=MESH)

    each_partner(greet)
    pl.semaphore_signal(barrier, inc=1, device_id=(after, me), device_id_type=MESH)
    pl.semaphore_signal(barrier, inc=1, device_id=(before, me), device_id_type=MESH)

    rel_copy = pltpu.make_async_copy(rel_hbm, rel_raw, rel_sem)
    rel_copy.start()

    def span(p):
        return pl.ds(pl.multiple_of(p * LANE, LANE), LANE)

    earlier = one_hot(iota((edges, edges), 0) < iota((edges, edges), 1))
    holder = iota((n, edges), 0)
    for s in range(SUBS):
        for t, ids_ref in enumerate((src_ref, dst_ref, neg_ref)):
            ids = ids_ref[s : s + 1, :]
            inside = (ids >= holder * rows) & (ids < holder * rows + rows)
            hits = jnp.where(inside, 1.0, 0.0)
            rank = dot(hits.astype(bf16), earlier)
            at = jnp.sum(
                hits * ((holder * LANE + t * cap).astype(f32) + rank), axis=0, keepdims=True
            )
            owner = jnp.sum(hits * holder.astype(f32), axis=0, keepdims=True)
            prow[s : s + 1, t * edges : (t + 1) * edges] = at
            lrow[s : s + 1, t * edges : (t + 1) * edges] = ids.astype(f32) - owner * rows

    def build_place_t(s):
        row = prow[s : s + 1, :].astype(jnp.int32)

        def body(p):
            place_t[span(p), :] = one_hot(iota((LANE, 3 * edges), 0) + p * LANE == row)

        each_index(body)

    def build_place(s):
        for t in range(3):
            column = to_column(prow[s : s + 1, t * edges : (t + 1) * edges]).astype(jnp.int32)

            def body(p):
                place[t * edges : (t + 1) * edges, span(p)] = one_hot(
                    iota((edges, LANE), 1) + p * LANE == column
                )

            each_index(body)

    def ask(s):
        local = lrow[s : s + 1, :]
        upper = iota((8, 3 * edges), 0)
        lhs = jnp.where(upper == 0, local, jnp.where(upper == 1, 1.0, 0.0)).astype(bf16)
        lane = iota((1, LANE), 1)
        offset = jnp.where(lane < cap, 0.0, float(rows))

        def wanted(p):
            found = dot(lhs, place_t[span(p), :], ((1,), (1,)))
            row = jnp.where(found[1:2] > 0.5, found[0:1] + offset, -1.0)
            return jnp.broadcast_to(row, (8, LANE))

        def body(p):
            wsend[s, p] = wanted(p)
            ask_copy(s, p).start()

        each_partner(body)
        wrecv[s, me] = wanted(me)

    def ask_copy(s, p):
        return pltpu.make_async_remote_copy(
            src_ref=wsend.at[s, p], dst_ref=wrecv.at[s, me],
            send_sem=wsem_s.at[s, p], recv_sem=wsem_r.at[s, me],
            device_id=(mb, p), device_id_type=MESH,
        )

    def ask_wait(s):
        def body(p):
            copy = pltpu.make_async_remote_copy(
                src_ref=wsend.at[s, p], dst_ref=wrecv.at[s, p],
                send_sem=wsem_s.at[s, p], recv_sem=wsem_r.at[s, p],
                device_id=(mb, p), device_id_type=MESH,
            )
            copy.wait()

        each_partner(body)

    def build_pick(s):
        def body(p):
            column = to_column(wrecv[s, p][0:1, :]).astype(jnp.int32)
            pick[span(p), :] = one_hot(iota((LANE, 2 * rows), 1) == column)

        each_index(body)

    def build_pick_t(s):
        def body(p):
            row = wrecv[s, p][0:1, :].astype(jnp.int32)
            pick_t[:, span(p)] = one_hot(iota((2 * rows, LANE), 0) == row)

        each_index(body)

    def pack(block, ref):
        for c in range(chunks):
            ref[c * slots : (c + 1) * slots, :] = block[:slots, c * LANE : (c + 1) * LANE].astype(bf16)
        ends = block[:, main:]
        total = ends[:PACK]
        for g in range(1, groups):
            total = total + pltpu.roll(ends[g * PACK : (g + 1) * PACK], g * tail, 1)
        ref[chunks * slots :, :] = total.astype(bf16)

    def exchange(k, make):
        def body(p):
            pack(make(p), msend.at[k, p])
            pltpu.make_async_remote_copy(
                src_ref=msend.at[k, p], dst_ref=mrecv.at[k, me],
                send_sem=msem_s.at[k, p], recv_sem=msem_r.at[k, me],
                device_id=(mb, p), device_id_type=MESH,
            ).start()

        each_partner(body)
        pack(make(me), mrecv.at[k, me])

    keep = iota((PACK, LANE), 1) < tail

    def collect(k):
        def unpack(p):
            at = pl.multiple_of(p * LANE, LANE)
            for c in range(chunks):
                flat[pl.ds(at, slots), c * LANE : (c + 1) * LANE] = mrecv[
                    k, p, c * slots : (c + 1) * slots, :
                ]
            ends = mrecv[k, p, chunks * slots : chunks * slots + PACK, :].astype(f32)
            for g in range(groups):
                part = ends if g == 0 else pltpu.roll(ends, LANE - g * tail, 1)
                flat[pl.ds(at + g * PACK, PACK), main:] = jnp.where(keep, part, 0.0).astype(bf16)

        unpack(me)

        def body(p):
            pltpu.make_async_remote_copy(
                src_ref=msend.at[k, p], dst_ref=mrecv.at[k, p],
                send_sem=msem_s.at[k, p], recv_sem=msem_r.at[k, p],
                device_id=(mb, p), device_id_type=MESH,
            ).wait()
            unpack(p)

        each_partner(body)

    def product(lhs_ref, first, count):
        depth = n * LANE
        step = min(depth, 1024)
        total = None
        for k in range(0, depth, step):
            part = dot(lhs_ref[first : first + count, k : k + step], flat[k : k + step, :])
            total = part if total is None else total + part
        return total

    build_place_t(0)
    pl.semaphore_wait(barrier, n + 1)
    ask(0)

    for buf, ref in ((lbuf, left_ref), (rbuf, right_ref)):
        buf[:, main:] = jnp.zeros((rows, LANE), f32)
        buf[:, :width] = ref[...]
    lcol[...] = jnp.broadcast_to(to_column(lstate_ref[...]), lcol.shape)
    rcol[...] = jnp.broadcast_to(to_column(rstate_ref[...]), rcol.shape)
    table[:rows, :] = lbuf[...].astype(bf16)
    table[rows:, :] = rbuf[...].astype(bf16)
    flat[...] = jnp.zeros(flat.shape, bf16)
    build_place_t(1)
    ask(1)

    rel_count = rel_raw.shape[0]

    def set_scale(s):
        column = to_column(kind_ref[s : s + 1, :].astype(f32)).astype(jnp.int32)
        chosen = one_hot(iota((edges, rel_count), 1) == column)
        scale[s] = dot(chosen, rel_hi[...]) + dot(chosen, rel_lo[...])

    for s in range(SUBS):
        if s == 0:
            ask_wait(0)
            build_pick(0)

        exchange(2 * s, lambda p: dot(pick[span(p), :], table[...]))

        build_place(s)
        build_place_t(s)
        build_pick_t(s)
        if s == 0:
            rel_copy.wait()
            for hi, lo in ((rel_hi, rel_lo),):
                hi[:, main:] = jnp.zeros((rel_count, LANE), bf16)
                lo[:, main:] = jnp.zeros((rel_count, LANE), bf16)
                raw = rel_raw[...]
                upper = raw.astype(bf16)
                hi[:, :width] = upper
                lo[:, :width] = (raw - upper.astype(f32)).astype(bf16)
            set_scale(0)
            set_scale(1)
            ask_wait(1)
            build_pick(1)

        collect(2 * s)
        for t in range(3):
            fetched[t * edges : (t + 1) * edges, :] = product(place, t * edges, edges)

        factor = scale[s]
        source = fetched[:edges, :] * factor
        goal = fetched[edges : 2 * edges, :]
        others = fetched[2 * edges :, :]
        inv_q = lax.rsqrt(jnp.sum(source * source, axis=1, keepdims=True) + tiny)
        inv_t = lax.rsqrt(jnp.sum(goal * goal, axis=1, keepdims=True) + tiny)
        inv_n = lax.rsqrt(jnp.sum(others * others, axis=1, keepdims=True) + tiny)
        query = source * inv_q
        target = goal * inv_t
        noise = others * inv_n
        query_half = query.astype(bf16)
        noise_half = noise.astype(bf16)
        positive = sharp * jnp.sum(query * target, axis=1, keepdims=True)
        scores = sharp * dot(query_half, noise_half, ((1,), (1,)))
        raised = jnp.exp(positive)
        spread = jnp.exp(scores)
        total = raised + jnp.sum(spread, axis=1, keepdims=True)
        miss = raised / total - 1.0
        weights = (spread / total).astype(bf16)
        query_grad = sharp * (miss * target + dot(weights, noise_half))
        noise_grad = sharp * dot(weights, query_half, ((0,), (0,)))
        along_q = jnp.sum(query * query_grad, axis=1, keepdims=True)
        along_n = jnp.sum(noise * noise_grad, axis=1, keepdims=True)
        grads[:edges, :] = ((query_grad - query * along_q) * inv_q * factor).astype(bf16)
        grads[edges : 2 * edges, :] = (
            (sharp * miss * query - target * (miss * positive)) * inv_t
        ).astype(bf16)
        grads[2 * edges :, :] = ((noise_grad - noise * along_n) * inv_n).astype(bf16)

        exchange(2 * s + 1, lambda p: dot(place_t[span(p), :], grads[...]))
        collect(2 * s + 1)

        for buf, col, first in ((rbuf, rcol, rows), (lbuf, lcol, 0)):
            grad = product(pick_t, first, rows)
            state = col[...][:, 0:1] + jnp.sum(grad * grad, axis=1, keepdims=True) * (1.0 / width)
            col[...] = jnp.broadcast_to(state, col.shape)
            new = buf[...] - rate * grad / (jnp.sqrt(state) + guard)
            buf[...] = new
            if s + 1 < SUBS:
                table[first : first + rows, :] = new.astype(bf16)
            elif first:
                deep = rows * tail // LANE
                for c in range(chunks):
                    ssend[c * rows : (c + 1) * rows, :] = new[:, c * LANE : (c + 1) * LANE]
                ends = new[:, main:]
                packed = ends[:deep]
                for g in range(1, LANE // tail):
                    packed = packed + pltpu.roll(ends[g * deep : (g + 1) * deep], g * tail, 1)
                base = chunks * rows
                ssend[base : base + deep, :] = packed
                base = base + deep
                for c in range(rows // LANE):
                    ssend[base + 8 * c : base + 8 * c + 8, :] = jnp.broadcast_to(
                        to_row(state[c * LANE : (c + 1) * LANE]), (8, LANE)
                    )
                shift = pltpu.make_async_remote_copy(
                    src_ref=ssend, dst_ref=srecv, send_sem=ssem.at[0], recv_sem=ssem.at[1],
                    device_id=(after, me), device_id_type=MESH,
                )
                shift.start()

    lout_ref[...] = lbuf[:, :width]
    lsout_ref[...] = to_row(lcol[...][:, 0:1])
    shift.wait()
    deep = rows * tail // LANE
    rout_ref[:, :main] = jnp.concatenate(
        [srecv[c * rows : (c + 1) * rows, :] for c in range(chunks)], axis=1
    )
    base = chunks * rows
    ends = srecv[base : base + deep, :]
    for g in range(LANE // tail):
        part = ends if g == 0 else pltpu.roll(ends, LANE - g * tail, 1)
        rout_ref[g * deep : (g + 1) * deep, main:] = part[:, :tail]
    base = base + deep
    for c in range(rows // LANE):
        rsout_ref[:, c * LANE : (c + 1) * LANE] = srecv[base + 8 * c : base + 8 * c + 1, :]


def on_device(
    left_emb, right_emb, left_state, right_state, relations, src_rows, dst_rows, rel_ids, neg_rows
):
    rows, width = left_emb.shape
    rel_count = relations.shape[0]
    n = lax.axis_size("edge")
    nb = lax.axis_size("bucket")
    edges = src_rows.shape[2]
    cap = edges // n + 4
    slots = -(-3 * cap // PACK) * PACK
    wide = -(-width // LANE) * LANE
    chunks = wide // LANE - 1
    message = chunks * slots + PACK
    shifted = chunks * rows + rows * (width - chunks * LANE) // LANE + 8 * (rows // LANE)
    vmem = pl.BlockSpec(memory_space=pltpu.VMEM)
    out = pl.pallas_call(
        functools.partial(kernel, n, nb, width, cap, slots),
        out_shape=(
            jax.ShapeDtypeStruct((rows, width), f32),
            jax.ShapeDtypeStruct((1, rows), f32),
            jax.ShapeDtypeStruct((rows, width), f32),
            jax.ShapeDtypeStruct((1, rows), f32),
        ),
        in_specs=[vmem] * 4 + [pl.BlockSpec(memory_space=pl.ANY)] + [vmem] * 4,
        out_specs=(vmem,) * 4,
        scratch_shapes=[
            pltpu.VMEM((rows, wide), f32),
            pltpu.VMEM((rows, wide), f32),
            pltpu.VMEM((rows, LANE), f32),
            pltpu.VMEM((rows, LANE), f32),
            pltpu.VMEM((2 * rows, wide), bf16),
            pltpu.VMEM((rel_count, width), f32),
            pltpu.VMEM((rel_count, wide), bf16),
            pltpu.VMEM((rel_count, wide), bf16),
            pltpu.VMEM((SUBS, edges, wide), f32),
            pltpu.VMEM((3 * edges, n * LANE), bf16),
            pltpu.VMEM((n * LANE, 3 * edges), bf16),
            pltpu.VMEM((n * LANE, 2 * rows), bf16),
            pltpu.VMEM((2 * rows, n * LANE), bf16),
            pltpu.VMEM((8, 3 * edges), f32),
            pltpu.VMEM((8, 3 * edges), f32),
            pltpu.VMEM((n * LANE, wide), bf16),
            pltpu.VMEM((3 * edges, wide), f32),
            pltpu.VMEM((3 * edges, wide), bf16),
            pltpu.VMEM((SUBS, n, 8, LANE), f32),
            pltpu.VMEM((SUBS, n, 8, LANE), f32),
            pltpu.VMEM((2 * SUBS, n, message, LANE), bf16),
            pltpu.VMEM((2 * SUBS, n, message, LANE), bf16),
            pltpu.VMEM((shifted, LANE), f32),
            pltpu.VMEM((shifted, LANE), f32),
            pltpu.SemaphoreType.DMA((SUBS, n)),
            pltpu.SemaphoreType.DMA((SUBS, n)),
            pltpu.SemaphoreType.DMA((2 * SUBS, n)),
            pltpu.SemaphoreType.DMA((2 * SUBS, n)),
            pltpu.SemaphoreType.DMA((2,)),
            pltpu.SemaphoreType.DMA,
        ],
        compiler_params=pltpu.CompilerParams(
            collective_id=0, has_side_effects=True, vmem_limit_bytes=56 * 1024 * 1024
        ),
    )(
        left_emb, right_emb, left_state.reshape(1, rows), right_state.reshape(1, rows),
        relations, src_rows[0], dst_rows[0], rel_ids[0], neg_rows[0],
    )
    return out[0], out[1].reshape(rows), out[2], out[3].reshape(rows)


def solution(mesh):
    return jax.shard_map(
        on_device,
        mesh=mesh,
        in_specs=(
            P(("bucket", "edge"), None),
            P(("bucket", "edge"), None),
            P(("bucket", "edge")),
            P(("bucket", "edge")),
            P(),
            P("bucket", None, "edge"),
            P("bucket", None, "edge"),
            P("bucket", None, "edge"),
            P("bucket", None, "edge"),
        ),
        out_specs=(
            P(("bucket", "edge"), None),
            P(("bucket", "edge")),
            P(("bucket", "edge"), None),
            P(("bucket", "edge")),
        ),
        check_vma=False,
    )
```

```python
import functools

import jax
import jax.numpy as jnp
from jax import lax
from jax.experimental import pallas as pl
from jax.experimental.pallas import tpu as pltpu
from jax.sharding import PartitionSpec as P

SUBS = 2
LANE = 128
PACK = 16

sharp = 40.0
rate = 0.5
tiny = 1e-06
guard = 1e-10

f32 = jnp.float32
bf16 = jnp.bfloat16
MESH = pl.DeviceIdType.MESH


def dot(first, second, dims=((1,), (0,))):
    return lax.dot_general(first, second, (dims, ((), ())), preferred_element_type=f32)


def iota(shape, dim):
    return lax.broadcasted_iota(jnp.int32, shape, dim)


def to_column(row):
    n = row.shape[1]
    same = iota((n, n), 0) == iota((n, n), 1)
    return jnp.sum(jnp.where(same, row, 0.0), axis=1, keepdims=True)


def to_row(column):
    n = column.shape[0]
    same = iota((n, n), 0) == iota((n, n), 1)
    return jnp.sum(jnp.where(same, column, 0.0), axis=0, keepdims=True)


def one_hot(where):
    return jnp.where(where, 1.0, 0.0).astype(bf16)


def kernel(
    n, nb, width, cap, slots,
    left_ref, right_ref, lstate_ref, rstate_ref, rel_hbm, src_ref, dst_ref, kind_ref, neg_ref,
    lout_ref, lsout_ref, rout_ref, rsout_ref,
    lbuf, rbuf, lcol, rcol, table, rel_raw, rel_hi, rel_lo, scale,
    place, place_t, pick, pick_t, prow, lrow, flat, fetched, grads,
    wsend, wrecv, msend, mrecv, base_send, base_recv, step_send, step_recv, hist_send, hist_recv,
    wsem_s, wsem_r, msem_s, msem_r, ssem, rel_sem,
):
    rows = left_ref.shape[1]
    edges = src_ref.shape[1]
    wide = lbuf.shape[1]
    main = wide - LANE
    tail = width - main
    groups = slots // PACK
    chunks = main // LANE
    me = lax.axis_index("edge")
    mb = lax.axis_index("bucket")
    after = lax.rem(mb + 1, nb)
    before = lax.rem(mb + nb - 1, nb)

    def partner(j):
        return lax.rem(me + n // 2 + ((j + 1) // 2) * (2 * (j % 2) - 1) + n, n)

    def each_partner(body):
        def step(j, carry):
            body(partner(j))
            return carry
        lax.fori_loop(0, n - 1, step, 0)

    def each_index(body):
        def step(j, carry):
            body(j)
            return carry
        lax.fori_loop(0, n, step, 0)

    barrier = pltpu.get_barrier_semaphore()

    def greet(p):
        pl.semaphore_signal(barrier, inc=1, device_id=(mb, p), device_id_type=MESH)

    each_partner(greet)
    pl.semaphore_signal(barrier, inc=1, device_id=(after, me), device_id_type=MESH)
    pl.semaphore_signal(barrier, inc=1, device_id=(before, me), device_id_type=MESH)

    rel_copy = pltpu.make_async_copy(rel_hbm, rel_raw, rel_sem)
    rel_copy.start()

    def onward(source, goal, i):
        return pltpu.make_async_remote_copy(
            src_ref=source, dst_ref=goal, send_sem=ssem.at[0, i], recv_sem=ssem.at[1, i],
            device_id=(after, me), device_id_type=MESH,
        )

    def span(p):
        return pl.ds(pl.multiple_of(p * LANE, LANE), LANE)

    earlier = one_hot(iota((edges, edges), 0) < iota((edges, edges), 1))
    holder = iota((n, edges), 0)
    for s in range(SUBS):
        for t, ids_ref in enumerate((src_ref, dst_ref, neg_ref)):
            ids = ids_ref[s : s + 1, :]
            inside = (ids >= holder * rows) & (ids < holder * rows + rows)
            hits = jnp.where(inside, 1.0, 0.0)
            rank = dot(hits.astype(bf16), earlier)
            at = jnp.sum(
                hits * ((holder * LANE + t * cap).astype(f32) + rank), axis=0, keepdims=True
            )
            owner = jnp.sum(hits * holder.astype(f32), axis=0, keepdims=True)
            prow[s : s + 1, t * edges : (t + 1) * edges] = at
            lrow[s : s + 1, t * edges : (t + 1) * edges] = ids.astype(f32) - owner * rows

    def build_place_t(s):
        row = prow[s : s + 1, :].astype(jnp.int32)

        def body(p):
            place_t[span(p), :] = one_hot(iota((LANE, 3 * edges), 0) + p * LANE == row)

        each_index(body)

    def build_place(s):
        for t in range(3):
            column = to_column(prow[s : s + 1, t * edges : (t + 1) * edges]).astype(jnp.int32)

            def body(p):
                place[t * edges : (t + 1) * edges, span(p)] = one_hot(
                    iota((edges, LANE), 1) + p * LANE == column
                )

            each_index(body)

    def ask(s):
        local = lrow[s : s + 1, :]
        upper = iota((8, 3 * edges), 0)
        lhs = jnp.where(upper == 0, local, jnp.where(upper == 1, 1.0, 0.0)).astype(bf16)
        lane = iota((1, LANE), 1)
        offset = jnp.where(lane < cap, 0.0, float(rows))

        def wanted(p):
            found = dot(lhs, place_t[span(p), :], ((1,), (1,)))
            row = jnp.where(found[1:2] > 0.5, found[0:1] + offset, -1.0)
            return jnp.broadcast_to(row, (8, LANE))

        def body(p):
            wsend[s, p] = wanted(p)
            ask_copy(s, p).start()

        each_partner(body)
        wrecv[s, me] = wanted(me)

    def ask_copy(s, p):
        return pltpu.make_async_remote_copy(
            src_ref=wsend.at[s, p], dst_ref=wrecv.at[s, me],
            send_sem=wsem_s.at[s, p], recv_sem=wsem_r.at[s, me],
            device_id=(mb, p), device_id_type=MESH,
        )

    def ask_wait(s):
        def body(p):
            copy = pltpu.make_async_remote_copy(
                src_ref=wsend.at[s, p], dst_ref=wrecv.at[s, p],
                send_sem=wsem_s.at[s, p], recv_sem=wsem_r.at[s, p],
                device_id=(mb, p), device_id_type=MESH,
            )
            copy.wait()

        each_partner(body)

    def build_pick(s):
        def body(p):
            column = to_column(wrecv[s, p][0:1, :]).astype(jnp.int32)
            pick[span(p), :] = one_hot(iota((LANE, 2 * rows), 1) == column)

        each_index(body)

    def build_pick_t(s):
        def body(p):
            row = wrecv[s, p][0:1, :].astype(jnp.int32)
            pick_t[:, span(p)] = one_hot(iota((2 * rows, LANE), 0) == row)

        each_index(body)

    def pack(block, ref):
        for c in range(chunks):
            ref[c * slots : (c + 1) * slots, :] = block[:slots, c * LANE : (c + 1) * LANE].astype(bf16)
        ends = block[:, main:]
        total = ends[:PACK]
        for g in range(1, groups):
            total = total + pltpu.roll(ends[g * PACK : (g + 1) * PACK], g * tail, 1)
        ref[chunks * slots :, :] = total.astype(bf16)

    def exchange(k, make):
        def body(p):
            pack(make(p), msend.at[k, p])
            pltpu.make_async_remote_copy(
                src_ref=msend.at[k, p], dst_ref=mrecv.at[k, me],
                send_sem=msem_s.at[k, p], recv_sem=msem_r.at[k, me],
                device_id=(mb, p), device_id_type=MESH,
            ).start()

        each_partner(body)
        pack(make(me), mrecv.at[k, me])

    keep = iota((PACK, LANE), 1) < tail

    def collect(k):
        def unpack(p):
            at = pl.multiple_of(p * LANE, LANE)
            for c in range(chunks):
                flat[pl.ds(at, slots), c * LANE : (c + 1) * LANE] = mrecv[
                    k, p, c * slots : (c + 1) * slots, :
                ]
            ends = mrecv[k, p, chunks * slots : chunks * slots + PACK, :].astype(f32)
            for g in range(groups):
                part = ends if g == 0 else pltpu.roll(ends, LANE - g * tail, 1)
                flat[pl.ds(at + g * PACK, PACK), main:] = jnp.where(keep, part, 0.0).astype(bf16)

        unpack(me)

        def body(p):
            pltpu.make_async_remote_copy(
                src_ref=msend.at[k, p], dst_ref=mrecv.at[k, p],
                send_sem=msem_s.at[k, p], recv_sem=msem_r.at[k, p],
                device_id=(mb, p), device_id_type=MESH,
            ).wait()
            unpack(p)

        each_partner(body)

    def product(lhs_ref, first, count):
        depth = n * LANE
        step = min(depth, 1024)
        total = None
        for k in range(0, depth, step):
            part = dot(lhs_ref[first : first + count, k : k + step], flat[k : k + step, :])
            total = part if total is None else total + part
        return total

    build_place_t(0)
    pl.semaphore_wait(barrier, n + 1)
    ask(0)

    for buf, ref in ((lbuf, left_ref), (rbuf, right_ref)):
        buf[...] = jnp.concatenate([ref[...], jnp.zeros((wide - width, rows), f32)], axis=0).T
    lcol[...] = jnp.broadcast_to(to_column(lstate_ref[...]), lcol.shape)
    rcol[...] = jnp.broadcast_to(to_column(rstate_ref[...]), rcol.shape)
    table[:rows, :] = lbuf[...].astype(bf16)
    table[rows:, :] = rbuf[...].astype(bf16)
    flat[...] = jnp.zeros(flat.shape, bf16)
    build_place_t(1)
    ask(1)

    rel_count = rel_raw.shape[1]

    def set_scale(s):
        column = to_column(kind_ref[s : s + 1, :].astype(f32)).astype(jnp.int32)
        chosen = one_hot(iota((edges, rel_count), 1) == column)
        last = ((1,), (1,))
        scale[s] = dot(chosen, rel_hi[...], last) + dot(chosen, rel_lo[...], last)

    for s in range(SUBS):
        if s == 0:
            ask_wait(0)
            build_pick(0)

        exchange(2 * s, lambda p: dot(pick[span(p), :], table[...]))

        if s == SUBS - 1:
            base_send[...] = rbuf[...].T[:width, :]
            onward(base_send, base_recv, 0).start()
        build_place(s)
        build_place_t(s)
        build_pick_t(s)
        if s == 0:
            rel_copy.wait()
            for ref in (rel_hi, rel_lo):
                ref[width:, :] = jnp.zeros((wide - width, rel_count), bf16)
            raw = rel_raw[...]
            upper = raw.astype(bf16)
            rel_hi[:width, :] = upper
            rel_lo[:width, :] = (raw - upper.astype(f32)).astype(bf16)
            set_scale(0)
            set_scale(1)
            ask_wait(1)
            build_pick(1)

        collect(2 * s)
        for t in range(3):
            fetched[t * edges : (t + 1) * edges, :] = product(place, t * edges, edges)

        factor = scale[s]
        source = fetched[:edges, :] * factor
        goal = fetched[edges : 2 * edges, :]
        others = fetched[2 * edges :, :]
        inv_q = lax.rsqrt(jnp.sum(source * source, axis=1, keepdims=True) + tiny)
        inv_t = lax.rsqrt(jnp.sum(goal * goal, axis=1, keepdims=True) + tiny)
        inv_n = lax.rsqrt(jnp.sum(others * others, axis=1, keepdims=True) + tiny)
        query = source * inv_q
        target = goal * inv_t
        noise = others * inv_n
        query_half = query.astype(bf16)
        noise_half = noise.astype(bf16)
        positive = sharp * jnp.sum(query * target, axis=1, keepdims=True)
        scores = sharp * dot(query_half, noise_half, ((1,), (1,)))
        raised = jnp.exp(positive)
        spread = jnp.exp(scores)
        total = raised + jnp.sum(spread, axis=1, keepdims=True)
        miss = raised / total - 1.0
        weights = (spread / total).astype(bf16)
        query_grad = sharp * (miss * target + dot(weights, noise_half))
        noise_grad = sharp * dot(weights, query_half, ((0,), (0,)))
        along_q = jnp.sum(query * query_grad, axis=1, keepdims=True)
        along_n = jnp.sum(noise * noise_grad, axis=1, keepdims=True)
        grads[:edges, :] = ((query_grad - query * along_q) * inv_q * factor).astype(bf16)
        grads[edges : 2 * edges, :] = (
            (sharp * miss * query - target * (miss * positive)) * inv_t
        ).astype(bf16)
        grads[2 * edges :, :] = ((noise_grad - noise * along_n) * inv_n).astype(bf16)

        exchange(2 * s + 1, lambda p: dot(place_t[span(p), :], grads[...]))
        collect(2 * s + 1)

        for buf, col, first in ((rbuf, rcol, rows), (lbuf, lcol, 0)):
            grad = product(pick_t, first, rows)
            state = col[...][:, 0:1] + jnp.sum(grad * grad, axis=1, keepdims=True) * (1.0 / width)
            col[...] = jnp.broadcast_to(state, col.shape)
            step = rate * grad / (jnp.sqrt(state) + guard)
            if s + 1 == SUBS and first:
                step_send[...] = step.T[:width, :].astype(bf16)
                onward(step_send, step_recv, 1).start()
                hist_send[...] = jnp.broadcast_to(to_row(state), hist_send.shape)
                onward(hist_send, hist_recv, 2).start()
            else:
                new = buf[...] - step
                buf[...] = new
                if s + 1 < SUBS:
                    table[first : first + rows, :] = new.astype(bf16)

    lout_ref[...] = lbuf[...].T[:width, :]
    lsout_ref[...] = to_row(lcol[...][:, 0:1])
    for i, (source, goal) in enumerate(
        ((base_send, base_recv), (step_send, step_recv), (hist_send, hist_recv))
    ):
        onward(source, goal, i).wait()
    rout_ref[...] = base_recv[...] - step_recv[...].astype(f32)
    rsout_ref[...] = hist_recv[0:1, :]


def finish(*refs):
    for i in range(4):
        refs[4 + i][...] = refs[i][...]


def on_device(
    left_emb, right_emb, left_state, right_state, relations, src_rows, dst_rows, rel_ids, neg_rows
):
    rows, width = left_emb.shape
    rel_count = relations.shape[0]
    n = lax.axis_size("edge")
    nb = lax.axis_size("bucket")
    edges = src_rows.shape[2]
    cap = edges // n + 4
    slots = -(-3 * cap // PACK) * PACK
    wide = -(-width // LANE) * LANE
    chunks = wide // LANE - 1
    message = chunks * slots + PACK
    vmem = pl.BlockSpec(memory_space=pltpu.VMEM)
    shapes = (
        jax.ShapeDtypeStruct((width, rows), f32),
        jax.ShapeDtypeStruct((1, rows), f32),
    ) * 2
    out = pl.pallas_call(
        functools.partial(kernel, n, nb, width, cap, slots),
        out_shape=shapes,
        in_specs=[vmem] * 4 + [pl.BlockSpec(memory_space=pl.ANY)] + [vmem] * 4,
        out_specs=(vmem,) * 4,
        scratch_shapes=[
            pltpu.VMEM((rows, wide), f32),
            pltpu.VMEM((rows, wide), f32),
            pltpu.VMEM((rows, LANE), f32),
            pltpu.VMEM((rows, LANE), f32),
            pltpu.VMEM((2 * rows, wide), bf16),
            pltpu.VMEM((width, rel_count), f32),
            pltpu.VMEM((wide, rel_count), bf16),
            pltpu.VMEM((wide, rel_count), bf16),
            pltpu.VMEM((SUBS, edges, wide), f32),
            pltpu.VMEM((3 * edges, n * LANE), bf16),
            pltpu.VMEM((n * LANE, 3 * edges), bf16),
            pltpu.VMEM((n * LANE, 2 * rows), bf16),
            pltpu.VMEM((2 * rows, n * LANE), bf16),
            pltpu.VMEM((8, 3 * edges), f32),
            pltpu.VMEM((8, 3 * edges), f32),
            pltpu.VMEM((n * LANE, wide), bf16),
            pltpu.VMEM((3 * edges, wide), f32),
            pltpu.VMEM((3 * edges, wide), bf16),
            pltpu.VMEM((SUBS, n, 8, LANE), f32),
            pltpu.VMEM((SUBS, n, 8, LANE), f32),
            pltpu.VMEM((2 * SUBS, n, message, LANE), bf16),
            pltpu.VMEM((2 * SUBS, n, message, LANE), bf16),
            pltpu.VMEM((width, rows), f32),
            pltpu.VMEM((width, rows), f32),
            pltpu.VMEM((width, rows), bf16),
            pltpu.VMEM((width, rows), bf16),
            pltpu.VMEM((8, rows), f32),
            pltpu.VMEM((8, rows), f32),
            pltpu.SemaphoreType.DMA((SUBS, n)),
            pltpu.SemaphoreType.DMA((SUBS, n)),
            pltpu.SemaphoreType.DMA((2 * SUBS, n)),
            pltpu.SemaphoreType.DMA((2 * SUBS, n)),
            pltpu.SemaphoreType.DMA((2, 3)),
            pltpu.SemaphoreType.DMA,
        ],
        compiler_params=pltpu.CompilerParams(
            collective_id=0, has_side_effects=True, vmem_limit_bytes=56 * 1024 * 1024
        ),
    )(
        left_emb.T, right_emb.T, left_state.reshape(1, rows), right_state.reshape(1, rows),
        relations.T, src_rows[0], dst_rows[0], rel_ids[0], neg_rows[0],
    )
    out = pl.pallas_call(
        finish, out_shape=shapes, in_specs=[vmem] * 4, out_specs=(vmem,) * 4
    )(*out)
    return out[0].T, out[1].reshape(rows), out[2].T, out[3].reshape(rows)


def solution(mesh):
    return jax.shard_map(
        on_device,
        mesh=mesh,
        in_specs=(
            P(("bucket", "edge"), None),
            P(("bucket", "edge"), None),
            P(("bucket", "edge")),
            P(("bucket", "edge")),
            P(),
            P("bucket", None, "edge"),
            P("bucket", None, "edge"),
            P("bucket", None, "edge"),
            P("bucket", None, "edge"),
        ),
        out_specs=(
            P(("bucket", "edge"), None),
            P(("bucket", "edge")),
            P(("bucket", "edge"), None),
            P(("bucket", "edge")),
        ),
        check_vma=False,
    )
```

```python
import functools

import jax
import jax.numpy as jnp
from jax import lax
from jax.experimental import pallas as pl
from jax.experimental.pallas import tpu as pltpu
from jax.sharding import PartitionSpec as P

SUBS = 2
LANE = 128
PACK = 16

sharp = 40.0
rate = 0.5
tiny = 1e-06
guard = 1e-10

f32 = jnp.float32
bf16 = jnp.bfloat16
MESH = pl.DeviceIdType.MESH


def dot(first, second, dims=((1,), (0,))):
    return lax.dot_general(first, second, (dims, ((), ())), preferred_element_type=f32)


def iota(shape, dim):
    return lax.broadcasted_iota(jnp.int32, shape, dim)


def to_column(row):
    n = row.shape[1]
    same = iota((n, n), 0) == iota((n, n), 1)
    return jnp.sum(jnp.where(same, row, 0.0), axis=1, keepdims=True)


def to_row(column):
    n = column.shape[0]
    same = iota((n, n), 0) == iota((n, n), 1)
    return jnp.sum(jnp.where(same, column, 0.0), axis=0, keepdims=True)


def one_hot(where):
    return jnp.where(where, 1.0, 0.0).astype(bf16)


def kernel(
    n, nb, width, cap, slots,
    left_ref, right_ref, lstate_ref, rstate_ref, rel_hbm, src_ref, dst_ref, kind_ref, neg_ref,
    lout_ref, lsout_ref, rout_ref, rsout_ref,
    lbuf, rbuf, lcol, rcol, table, rel_raw, rel_hi, rel_lo, scale,
    place, place_t, pick, pick_t, prow, lrow, flat, fetched, grads,
    wsend, wrecv, msend, mrecv, base_send, base_recv, step_send, step_recv, hist_send, hist_recv,
    wsem_s, wsem_r, msem_s, msem_r, ssem, rel_sem,
):
    rows = left_ref.shape[1]
    edges = src_ref.shape[1]
    wide = lbuf.shape[1]
    main = wide - LANE
    tail = width - main
    groups = slots // PACK
    chunks = main // LANE
    me = lax.axis_index("edge")
    mb = lax.axis_index("bucket")
    after = lax.rem(mb + 1, nb)
    before = lax.rem(mb + nb - 1, nb)

    half = n // 2
    mine = (me // half) * half
    other = half - mine

    def far(j):
        return other + lax.rem(me + j, half)

    def near(j):
        return mine + lax.rem(me + j, half)

    def each_far(body):
        def step(j, carry):
            body(far(j))
            return carry
        lax.fori_loop(0, half, step, 0)

    def each_near(body):
        def step(j, carry):
            body(near(j))
            return carry
        lax.fori_loop(1, half, step, 0)

    def each_partner(body):
        each_far(body)
        each_near(body)

    def each_index(body):
        def step(j, carry):
            body(j)
            return carry
        lax.fori_loop(0, n, step, 0)

    barrier = pltpu.get_barrier_semaphore()

    def greet(p):
        pl.semaphore_signal(barrier, inc=1, device_id=(mb, p), device_id_type=MESH)

    each_partner(greet)
    pl.semaphore_signal(barrier, inc=1, device_id=(after, me), device_id_type=MESH)
    pl.semaphore_signal(barrier, inc=1, device_id=(before, me), device_id_type=MESH)

    rel_copy = pltpu.make_async_copy(rel_hbm, rel_raw, rel_sem)
    rel_copy.start()

    def onward(source, goal, i):
        return pltpu.make_async_remote_copy(
            src_ref=source, dst_ref=goal, send_sem=ssem.at[0, i], recv_sem=ssem.at[1, i],
            device_id=(after, me), device_id_type=MESH,
        )

    def span(p):
        return pl.ds(pl.multiple_of(p * LANE, LANE), LANE)

    earlier = one_hot(iota((edges, edges), 0) < iota((edges, edges), 1))
    holder = iota((n, edges), 0)
    for s in range(SUBS):
        for t, ids_ref in enumerate((src_ref, dst_ref, neg_ref)):
            ids = ids_ref[s : s + 1, :]
            inside = (ids >= holder * rows) & (ids < holder * rows + rows)
            hits = jnp.where(inside, 1.0, 0.0)
            rank = dot(hits.astype(bf16), earlier)
            at = jnp.sum(
                hits * ((holder * LANE + t * cap).astype(f32) + rank), axis=0, keepdims=True
            )
            owner = jnp.sum(hits * holder.astype(f32), axis=0, keepdims=True)
            prow[s : s + 1, t * edges : (t + 1) * edges] = at
            lrow[s : s + 1, t * edges : (t + 1) * edges] = ids.astype(f32) - owner * rows

    def build_place_t(s):
        row = prow[s : s + 1, :].astype(jnp.int32)

        def body(p):
            place_t[span(p), :] = one_hot(iota((LANE, 3 * edges), 0) + p * LANE == row)

        each_index(body)

    def build_place(s):
        for t in range(3):
            column = to_column(prow[s : s + 1, t * edges : (t + 1) * edges]).astype(jnp.int32)

            def body(p):
                place[t * edges : (t + 1) * edges, span(p)] = one_hot(
                    iota((edges, LANE), 1) + p * LANE == column
                )

            each_index(body)

    def ask(s):
        local = lrow[s : s + 1, :]
        upper = iota((8, 3 * edges), 0)
        lhs = jnp.where(upper == 0, local, jnp.where(upper == 1, 1.0, 0.0)).astype(bf16)
        lane = iota((1, LANE), 1)
        offset = jnp.where(lane < cap, 0.0, float(rows))

        found = dot(lhs, place_t[...], ((1,), (1,)))
        for p in range(n):
            part = found[:, p * LANE : (p + 1) * LANE]
            row = jnp.where(part[1:2] > 0.5, part[0:1] + offset, -1.0)
            wsend[s, p] = jnp.broadcast_to(row, (8, LANE))

        each_partner(lambda p: ask_copy(s, p).start())
        wrecv[s, me] = wsend[s, me]

    def ask_copy(s, p):
        return pltpu.make_async_remote_copy(
            src_ref=wsend.at[s, p], dst_ref=wrecv.at[s, me],
            send_sem=wsem_s.at[s, p], recv_sem=wsem_r.at[s, me],
            device_id=(mb, p), device_id_type=MESH,
        )

    def ask_wait(s):
        def body(p):
            copy = pltpu.make_async_remote_copy(
                src_ref=wsend.at[s, p], dst_ref=wrecv.at[s, p],
                send_sem=wsem_s.at[s, p], recv_sem=wsem_r.at[s, p],
                device_id=(mb, p), device_id_type=MESH,
            )
            copy.wait()

        each_partner(body)

    def build_pick(s):
        def body(p):
            column = to_column(wrecv[s, p][0:1, :]).astype(jnp.int32)
            pick[span(p), :] = one_hot(iota((LANE, 2 * rows), 1) == column)

        each_index(body)

    def build_pick_t(s):
        def body(p):
            row = wrecv[s, p][0:1, :].astype(jnp.int32)
            pick_t[:, span(p)] = one_hot(iota((2 * rows, LANE), 0) == row)

        each_index(body)

    full = cap // PACK
    some = -(-cap // PACK)
    height = chunks * PACK
    cut_rows = (full * height, some * height + PACK)

    def group_at(g):
        return g * height + (PACK if g >= some else 0)

    def pack(block, ref, first, count, ends_too):
        for g in range(first, count):
            for c in range(chunks):
                at = group_at(g) + c * PACK
                ref[at : at + PACK, :] = block[
                    g * PACK : (g + 1) * PACK, c * LANE : (c + 1) * LANE
                ].astype(bf16)
        if ends_too:
            ends = block[:, main:]
            total = ends[:PACK]
            for g in range(1, groups):
                total = total + pltpu.roll(ends[g * PACK : (g + 1) * PACK], g * tail, 1)
            ref[some * height : some * height + PACK, :] = total.astype(bf16)

    def piece(k, p, part, slot):
        cut_at = cut_rows[k % 2]
        lines = pl.ds(0, cut_at) if part == 0 else pl.ds(cut_at, groups * height + PACK - cut_at)
        return pltpu.make_async_remote_copy(
            src_ref=msend.at[k, p, lines], dst_ref=mrecv.at[k, slot, lines],
            send_sem=msem_s.at[k, part, p], recv_sem=msem_r.at[k, part, slot],
            device_id=(mb, p), device_id_type=MESH,
        )

    def start(k, p, part):
        if cut_rows[k % 2] > 0 or part == 1:
            piece(k, p, part, me).start()

    def finished(k, p, part):
        if cut_rows[k % 2] > 0 or part == 1:
            piece(k, p, part, p).wait()

    keep = iota((PACK, LANE), 1) < tail

    def unpack(k, p, first, count, ends_too):
        at = pl.multiple_of(p * LANE, LANE)
        for g in range(first, count):
            for c in range(chunks):
                line = group_at(g) + c * PACK
                flat[pl.ds(at + g * PACK, PACK), c * LANE : (c + 1) * LANE] = mrecv[
                    k, p, line : line + PACK, :
                ]
        if ends_too:
            ends = mrecv[k, p, some * height : some * height + PACK, :].astype(f32)
            for g in range(groups):
                part = ends if g == 0 else pltpu.roll(ends, LANE - g * tail, 1)
                flat[pl.ds(at + g * PACK, PACK), main:] = jnp.where(keep, part, 0.0).astype(bf16)

    def half_span(first):
        return pl.ds(pl.multiple_of(first * LANE, LANE * half), LANE * half)

    def product(lhs_ref, first, count, start_at):
        lines = half_span(start_at)
        return dot(lhs_ref[first : first + count, lines], flat[lines, :])

    def reply_all(k):
        def body(p):
            block = dot(pick[span(p), :], table[...])
            pack(block, msend.at[k, p], 0, groups, True)
            start(k, p, 0)
            start(k, p, 1)

        each_partner(body)
        pack(dot(pick[span(me), :], table[...]), mrecv.at[k, me], 0, groups, True)

    def reply_first(k):
        def block(p):
            lines = pl.ds(pl.multiple_of(p * LANE, LANE), full * PACK)
            return dot(pick[lines, :rows], table[:rows, :])

        def body(p):
            pack(block(p), msend.at[k, p], 0, full, False)
            start(k, p, 0)

        if full:
            each_partner(body)
            pack(block(me), mrecv.at[k, me], 0, full, False)

    def reply_rest(k):
        def body(p):
            pack(dot(pick[span(p), :], table[...]), msend.at[k, p], full, groups, True)
            start(k, p, 1)

        each_partner(body)
        pack(dot(pick[span(me), :], table[...]), mrecv.at[k, me], full, groups, True)

    def fetch(k):
        def body(p):
            finished(k, p, 0)
            finished(k, p, 1)
            unpack(k, p, 0, groups, True)

        unpack(k, me, 0, groups, True)
        each_near(body)
        for t in range(3):
            fetched[t * edges : (t + 1) * edges, :] = product(place, t * edges, edges, mine)
        each_far(body)
        for t in range(3):
            fetched[t * edges : (t + 1) * edges, :] += product(place, t * edges, edges, other)

    def give(k):
        def body(p):
            block = dot(place_t[span(p), :], grads[...])
            pack(block, msend.at[k, p], 0, groups, True)
            start(k, p, 0)

        each_partner(body)
        each_partner(lambda p: start(k, p, 1))
        pack(dot(place_t[span(me), :], grads[...]), mrecv.at[k, me], 0, groups, True)

    def take(k, part, first):
        lo, hi = ((0, some), (some, groups))[part]

        def body(p):
            finished(k, p, part)
            unpack(k, p, lo, hi, part == 0)

        unpack(k, me, lo, hi, part == 0)
        each_near(body)
        total = product(pick_t, first, rows, mine)
        each_far(body)
        return total + product(pick_t, first, rows, other)

    build_place_t(0)
    pl.semaphore_wait(barrier, n + 1)
    ask(0)

    for buf, ref in ((lbuf, left_ref), (rbuf, right_ref)):
        buf[...] = jnp.concatenate([ref[...], jnp.zeros((wide - width, rows), f32)], axis=0).T
    lcol[...] = jnp.broadcast_to(to_column(lstate_ref[...]), lcol.shape)
    rcol[...] = jnp.broadcast_to(to_column(rstate_ref[...]), rcol.shape)
    table[:rows, :] = lbuf[...].astype(bf16)
    table[rows:, :] = rbuf[...].astype(bf16)
    flat[...] = jnp.zeros(flat.shape, bf16)
    build_place_t(1)
    ask(1)

    rel_count = rel_raw.shape[1]

    def set_scale(s):
        column = to_column(kind_ref[s : s + 1, :].astype(f32)).astype(jnp.int32)
        chosen = one_hot(iota((edges, rel_count), 1) == column)
        last = ((1,), (1,))
        scale[s] = dot(chosen, rel_hi[...], last) + dot(chosen, rel_lo[...], last)

    for s in range(SUBS):
        if s == 0:
            ask_wait(0)
            build_pick(0)

            reply_all(0)

        if s == SUBS - 1:
            base_send[...] = rbuf[...].T[:width, :]
            onward(base_send, base_recv, 0).start()
        build_place(s)
        build_place_t(s)
        build_pick_t(s)
        if s == 0:
            rel_copy.wait()
            for ref in (rel_hi, rel_lo):
                ref[width:, :] = jnp.zeros((wide - width, rel_count), bf16)
            raw = rel_raw[...]
            upper = raw.astype(bf16)
            rel_hi[:width, :] = upper
            rel_lo[:width, :] = (raw - upper.astype(f32)).astype(bf16)
            set_scale(0)
            set_scale(1)
            ask_wait(1)
            build_pick(1)

        fetch(2 * s)
        factor = scale[s]
        source = fetched[:edges, :] * factor
        goal = fetched[edges : 2 * edges, :]
        others = fetched[2 * edges :, :]
        inv_q = lax.rsqrt(jnp.sum(source * source, axis=1, keepdims=True) + tiny)
        inv_t = lax.rsqrt(jnp.sum(goal * goal, axis=1, keepdims=True) + tiny)
        inv_n = lax.rsqrt(jnp.sum(others * others, axis=1, keepdims=True) + tiny)
        query = source * inv_q
        target = goal * inv_t
        noise = others * inv_n
        query_half = query.astype(bf16)
        noise_half = noise.astype(bf16)
        positive = sharp * jnp.sum(query * target, axis=1, keepdims=True)
        scores = sharp * dot(query_half, noise_half, ((1,), (1,)))
        raised = jnp.exp(positive)
        spread = jnp.exp(scores)
        total = raised + jnp.sum(spread, axis=1, keepdims=True)
        miss = raised / total - 1.0
        weights = (spread / total).astype(bf16)
        query_grad = sharp * (miss * target + dot(weights, noise_half))
        noise_grad = sharp * dot(weights, query_half, ((0,), (0,)))
        along_q = jnp.sum(query * query_grad, axis=1, keepdims=True)
        along_n = jnp.sum(noise * noise_grad, axis=1, keepdims=True)
        grads[:edges, :] = ((query_grad - query * along_q) * inv_q * factor).astype(bf16)
        grads[edges : 2 * edges, :] = (
            (sharp * miss * query - target * (miss * positive)) * inv_t
        ).astype(bf16)
        grads[2 * edges :, :] = ((noise_grad - noise * along_n) * inv_n).astype(bf16)

        give(2 * s + 1)
        for part, (buf, col, first) in enumerate(((lbuf, lcol, 0), (rbuf, rcol, rows))):
            grad = take(2 * s + 1, part, first)
            state = col[...][:, 0:1] + jnp.sum(grad * grad, axis=1, keepdims=True) * (1.0 / width)
            col[...] = jnp.broadcast_to(state, col.shape)
            step = rate * grad / (jnp.sqrt(state) + guard)
            if s + 1 == SUBS and first:
                step_send[...] = step.T[:width, :].astype(bf16)
                onward(step_send, step_recv, 1).start()
                hist_send[...] = jnp.broadcast_to(to_row(state), hist_send.shape)
                onward(hist_send, hist_recv, 2).start()
            else:
                new = buf[...] - step
                buf[...] = new
                if s + 1 < SUBS:
                    table[first : first + rows, :] = new.astype(bf16)
                    (reply_rest if part else reply_first)(2 * s + 2)

    lout_ref[...] = lbuf[...].T[:width, :]
    lsout_ref[...] = to_row(lcol[...][:, 0:1])
    for i, (source, goal) in enumerate(
        ((base_send, base_recv), (step_send, step_recv), (hist_send, hist_recv))
    ):
        onward(source, goal, i).wait()
    rout_ref[...] = base_recv[...] - step_recv[...].astype(f32)
    rsout_ref[...] = hist_recv[0:1, :]


def finish(*refs):
    for i in range(4):
        refs[4 + i][...] = refs[i][...]


def on_device(
    left_emb, right_emb, left_state, right_state, relations, src_rows, dst_rows, rel_ids, neg_rows
):
    rows, width = left_emb.shape
    rel_count = relations.shape[0]
    n = lax.axis_size("edge")
    nb = lax.axis_size("bucket")
    edges = src_rows.shape[2]
    cap = edges // n + 4
    slots = -(-3 * cap // PACK) * PACK
    wide = -(-width // LANE) * LANE
    chunks = wide // LANE - 1
    message = chunks * slots + PACK
    vmem = pl.BlockSpec(memory_space=pltpu.VMEM)
    shapes = (
        jax.ShapeDtypeStruct((width, rows), f32),
        jax.ShapeDtypeStruct((1, rows), f32),
    ) * 2
    out = pl.pallas_call(
        functools.partial(kernel, n, nb, width, cap, slots),
        out_shape=shapes,
        in_specs=[vmem] * 4 + [pl.BlockSpec(memory_space=pl.ANY)] + [vmem] * 4,
        out_specs=(vmem,) * 4,
        scratch_shapes=[
            pltpu.VMEM((rows, wide), f32),
            pltpu.VMEM((rows, wide), f32),
            pltpu.VMEM((rows, LANE), f32),
            pltpu.VMEM((rows, LANE), f32),
            pltpu.VMEM((2 * rows, wide), bf16),
            pltpu.VMEM((width, rel_count), f32),
            pltpu.VMEM((wide, rel_count), bf16),
            pltpu.VMEM((wide, rel_count), bf16),
            pltpu.VMEM((SUBS, edges, wide), f32),
            pltpu.VMEM((3 * edges, n * LANE), bf16),
            pltpu.VMEM((n * LANE, 3 * edges), bf16),
            pltpu.VMEM((n * LANE, 2 * rows), bf16),
            pltpu.VMEM((2 * rows, n * LANE), bf16),
            pltpu.VMEM((8, 3 * edges), f32),
            pltpu.VMEM((8, 3 * edges), f32),
            pltpu.VMEM((n * LANE, wide), bf16),
            pltpu.VMEM((3 * edges, wide), f32),
            pltpu.VMEM((3 * edges, wide), bf16),
            pltpu.VMEM((SUBS, n, 8, LANE), f32),
            pltpu.VMEM((SUBS, n, 8, LANE), f32),
            pltpu.VMEM((2 * SUBS, n, message, LANE), bf16),
            pltpu.VMEM((2 * SUBS, n, message, LANE), bf16),
            pltpu.VMEM((width, rows), f32),
            pltpu.VMEM((width, rows), f32),
            pltpu.VMEM((width, rows), bf16),
            pltpu.VMEM((width, rows), bf16),
            pltpu.VMEM((8, rows), f32),
            pltpu.VMEM((8, rows), f32),
            pltpu.SemaphoreType.DMA((SUBS, n)),
            pltpu.SemaphoreType.DMA((SUBS, n)),
            pltpu.SemaphoreType.DMA((2 * SUBS, 2, n)),
            pltpu.SemaphoreType.DMA((2 * SUBS, 2, n)),
            pltpu.SemaphoreType.DMA((2, 3)),
            pltpu.SemaphoreType.DMA,
        ],
        compiler_params=pltpu.CompilerParams(
            collective_id=0, has_side_effects=True, vmem_limit_bytes=56 * 1024 * 1024
        ),
    )(
        left_emb.T, right_emb.T, left_state.reshape(1, rows), right_state.reshape(1, rows),
        relations.T, src_rows[0], dst_rows[0], rel_ids[0], neg_rows[0],
    )
    out = pl.pallas_call(
        finish, out_shape=shapes, in_specs=[vmem] * 4, out_specs=(vmem,) * 4
    )(*out)
    return out[0].T, out[1].reshape(rows), out[2].T, out[3].reshape(rows)


def solution(mesh):
    return jax.shard_map(
        on_device,
        mesh=mesh,
        in_specs=(
            P(("bucket", "edge"), None),
            P(("bucket", "edge"), None),
            P(("bucket", "edge")),
            P(("bucket", "edge")),
            P(),
            P("bucket", None, "edge"),
            P("bucket", None, "edge"),
            P("bucket", None, "edge"),
            P("bucket", None, "edge"),
        ),
        out_specs=(
            P(("bucket", "edge"), None),
            P(("bucket", "edge")),
            P(("bucket", "edge"), None),
            P(("bucket", "edge")),
        ),
        check_vma=False,
    )
```

```python
import functools

import jax
import jax.numpy as jnp
from jax import lax
from jax.experimental import pallas as pl
from jax.experimental.pallas import tpu as pltpu
from jax.sharding import PartitionSpec as P

SUBS = 2
LANE = 128
PACK = 16

sharp = 40.0
rate = 0.5
tiny = 1e-06
guard = 1e-10

f32 = jnp.float32
bf16 = jnp.bfloat16
MESH = pl.DeviceIdType.MESH


def dot(first, second, dims=((1,), (0,))):
    return lax.dot_general(first, second, (dims, ((), ())), preferred_element_type=f32)


def iota(shape, dim):
    return lax.broadcasted_iota(jnp.int32, shape, dim)


def to_column(row):
    n = row.shape[1]
    same = iota((n, n), 0) == iota((n, n), 1)
    return jnp.sum(jnp.where(same, row, 0.0), axis=1, keepdims=True)


def to_row(column):
    n = column.shape[0]
    same = iota((n, n), 0) == iota((n, n), 1)
    return jnp.sum(jnp.where(same, column, 0.0), axis=0, keepdims=True)


def one_hot(where):
    return jnp.where(where, 1.0, 0.0).astype(bf16)


def kernel(
    n, nb, width, cap, slots,
    left_ref, right_ref, lstate_ref, rstate_ref, rel_hbm, src_ref, dst_ref, kind_ref, neg_ref,
    lout_ref, lsout_ref, rout_ref, rsout_ref,
    lbuf, rbuf, lcol, rcol, table, rel_raw, rel_hi, rel_lo, scale,
    place, place_t, pick, pick_t, prow, lrow, flat, fetched, grads,
    wsend, wrecv, msend, mrecv, base_send, base_recv, step_send, step_recv, hist_send, hist_recv,
    wsem_s, wsem_r, msem_s, msem_r, ssem, rel_sem,
):
    rows = left_ref.shape[1]
    edges = src_ref.shape[1]
    wide = lbuf.shape[1]
    main = wide - LANE
    tail = width - main
    groups = slots // PACK
    chunks = main // LANE
    me = lax.axis_index("edge")
    mb = lax.axis_index("bucket")
    after = lax.rem(mb + 1, nb)
    before = lax.rem(mb + nb - 1, nb)

    half = n // 2
    mine = (me // half) * half
    other = half - mine

    def far(j):
        return other + lax.rem(me + j, half)

    def near(j):
        return mine + lax.rem(me + j, half)

    def each_far(body):
        def step(j, carry):
            body(far(j))
            return carry
        lax.fori_loop(0, half, step, 0)

    def each_near(body):
        def step(j, carry):
            body(near(j))
            return carry
        lax.fori_loop(1, half, step, 0)

    def each_partner(body):
        def step(j, carry):
            turn = n // 2 + ((j + 1) // 2) * (2 * (j % 2) - 1)
            body(lax.rem(me + turn + n, n))
            return carry
        lax.fori_loop(0, n - 1, step, 0)

    def each_index(body):
        def step(j, carry):
            body(j)
            return carry
        lax.fori_loop(0, n, step, 0)

    barrier = pltpu.get_barrier_semaphore()

    def greet(p):
        pl.semaphore_signal(barrier, inc=1, device_id=(mb, p), device_id_type=MESH)

    each_partner(greet)
    pl.semaphore_signal(barrier, inc=1, device_id=(after, me), device_id_type=MESH)
    pl.semaphore_signal(barrier, inc=1, device_id=(before, me), device_id_type=MESH)

    rel_copy = pltpu.make_async_copy(rel_hbm, rel_raw, rel_sem)
    rel_copy.start()

    def onward(source, goal, i):
        return pltpu.make_async_remote_copy(
            src_ref=source, dst_ref=goal, send_sem=ssem.at[0, i], recv_sem=ssem.at[1, i],
            device_id=(after, me), device_id_type=MESH,
        )

    def span(p):
        return pl.ds(pl.multiple_of(p * LANE, LANE), LANE)

    earlier = one_hot(iota((edges, edges), 0) < iota((edges, edges), 1))
    holder = iota((n, edges), 0)
    for s in range(SUBS):
        for t, ids_ref in enumerate((src_ref, dst_ref, neg_ref)):
            ids = ids_ref[s : s + 1, :]
            inside = (ids >= holder * rows) & (ids < holder * rows + rows)
            hits = jnp.where(inside, 1.0, 0.0)
            rank = dot(hits.astype(bf16), earlier)
            at = jnp.sum(
                hits * ((holder * LANE + t * cap).astype(f32) + rank), axis=0, keepdims=True
            )
            owner = jnp.sum(hits * holder.astype(f32), axis=0, keepdims=True)
            prow[s : s + 1, t * edges : (t + 1) * edges] = at
            lrow[s : s + 1, t * edges : (t + 1) * edges] = ids.astype(f32) - owner * rows

    def build_place_t(s):
        row = prow[s : s + 1, :].astype(jnp.int32)

        def body(p):
            place_t[span(p), :] = one_hot(iota((LANE, 3 * edges), 0) + p * LANE == row)

        each_index(body)

    def build_place(s):
        for t in range(3):
            column = to_column(prow[s : s + 1, t * edges : (t + 1) * edges]).astype(jnp.int32)

            def body(p):
                place[t * edges : (t + 1) * edges, span(p)] = one_hot(
                    iota((edges, LANE), 1) + p * LANE == column
                )

            each_index(body)

    def ask(s):
        local = lrow[s : s + 1, :]
        upper = iota((8, 3 * edges), 0)
        lhs = jnp.where(upper == 0, local, jnp.where(upper == 1, 1.0, 0.0)).astype(bf16)
        lane = iota((1, LANE), 1)
        offset = jnp.where(lane < cap, 0.0, float(rows))

        found = dot(lhs, place_t[...], ((1,), (1,)))
        for p in range(n):
            part = found[:, p * LANE : (p + 1) * LANE]
            row = jnp.where(part[1:2] > 0.5, part[0:1] + offset, -1.0)
            wsend[s, p] = jnp.broadcast_to(row, (8, LANE))

        each_partner(lambda p: ask_copy(s, p).start())
        wrecv[s, me] = wsend[s, me]

    def ask_copy(s, p):
        return pltpu.make_async_remote_copy(
            src_ref=wsend.at[s, p], dst_ref=wrecv.at[s, me],
            send_sem=wsem_s.at[s, p], recv_sem=wsem_r.at[s, me],
            device_id=(mb, p), device_id_type=MESH,
        )

    def ask_wait(s):
        def body(p):
            copy = pltpu.make_async_remote_copy(
                src_ref=wsend.at[s, p], dst_ref=wrecv.at[s, p],
                send_sem=wsem_s.at[s, p], recv_sem=wsem_r.at[s, p],
                device_id=(mb, p), device_id_type=MESH,
            )
            copy.wait()

        each_partner(body)

    def build_pick(s):
        def body(p):
            column = to_column(wrecv[s, p][0:1, :]).astype(jnp.int32)
            pick[span(p), :] = one_hot(iota((LANE, 2 * rows), 1) == column)

        each_index(body)

    def build_pick_t(s):
        def body(p):
            row = wrecv[s, p][0:1, :].astype(jnp.int32)
            pick_t[:, span(p)] = one_hot(iota((2 * rows, LANE), 0) == row)

        each_index(body)

    full = cap // PACK
    some = -(-cap // PACK)
    height = chunks * PACK
    cut_rows = (full * height, some * height + PACK)

    def group_at(g):
        return g * height + (PACK if g >= some else 0)

    def pack(block, ref, first, count, ends_too):
        for g in range(first, count):
            for c in range(chunks):
                at = group_at(g) + c * PACK
                ref[at : at + PACK, :] = block[
                    g * PACK : (g + 1) * PACK, c * LANE : (c + 1) * LANE
                ].astype(bf16)
        if ends_too:
            ends = block[:, main:]
            total = ends[:PACK]
            for g in range(1, groups):
                total = total + pltpu.roll(ends[g * PACK : (g + 1) * PACK], g * tail, 1)
            ref[some * height : some * height + PACK, :] = total.astype(bf16)

    def piece(k, p, part, slot):
        cut_at = cut_rows[k % 2]
        lines = pl.ds(0, cut_at) if part == 0 else pl.ds(cut_at, groups * height + PACK - cut_at)
        return pltpu.make_async_remote_copy(
            src_ref=msend.at[k, p, lines], dst_ref=mrecv.at[k, slot, lines],
            send_sem=msem_s.at[k, part, p], recv_sem=msem_r.at[k, part, slot],
            device_id=(mb, p), device_id_type=MESH,
        )

    def start(k, p, part):
        if cut_rows[k % 2] > 0 or part == 1:
            piece(k, p, part, me).start()

    def finished(k, p, part):
        if cut_rows[k % 2] > 0 or part == 1:
            piece(k, p, part, p).wait()

    keep = iota((PACK, LANE), 1) < tail

    def unpack(k, p, first, count, ends_too):
        at = pl.multiple_of(p * LANE, LANE)
        for g in range(first, count):
            for c in range(chunks):
                line = group_at(g) + c * PACK
                flat[pl.ds(at + g * PACK, PACK), c * LANE : (c + 1) * LANE] = mrecv[
                    k, p, line : line + PACK, :
                ]
        if ends_too:
            ends = mrecv[k, p, some * height : some * height + PACK, :].astype(f32)
            for g in range(groups):
                part = ends if g == 0 else pltpu.roll(ends, LANE - g * tail, 1)
                flat[pl.ds(at + g * PACK, PACK), main:] = jnp.where(keep, part, 0.0).astype(bf16)

    def half_span(first):
        return pl.ds(pl.multiple_of(first * LANE, LANE * half), LANE * half)

    def product(lhs_ref, first, count, start_at):
        lines = half_span(start_at)
        return dot(lhs_ref[first : first + count, lines], flat[lines, :])

    def reply_all(k):
        def body(p):
            block = dot(pick[span(p), :], table[...])
            pack(block, msend.at[k, p], 0, groups, True)
            start(k, p, 0)
            start(k, p, 1)

        each_partner(body)
        pack(dot(pick[span(me), :], table[...]), mrecv.at[k, me], 0, groups, True)

    def reply_first(k):
        def block(p):
            lines = pl.ds(pl.multiple_of(p * LANE, LANE), full * PACK)
            return dot(pick[lines, :rows], table[:rows, :])

        def body(p):
            pack(block(p), msend.at[k, p], 0, full, False)
            start(k, p, 0)

        if full:
            each_partner(body)
            pack(block(me), mrecv.at[k, me], 0, full, False)

    def reply_rest(k):
        def body(p):
            pack(dot(pick[span(p), :], table[...]), msend.at[k, p], full, groups, True)
            start(k, p, 1)

        each_partner(body)
        pack(dot(pick[span(me), :], table[...]), mrecv.at[k, me], full, groups, True)

    def fetch(k):
        def body(p):
            finished(k, p, 0)
            finished(k, p, 1)
            unpack(k, p, 0, groups, True)

        unpack(k, me, 0, groups, True)
        each_near(body)
        for t in range(3):
            fetched[t * edges : (t + 1) * edges, :] = product(place, t * edges, edges, mine)
        each_far(body)
        for t in range(3):
            fetched[t * edges : (t + 1) * edges, :] += product(place, t * edges, edges, other)

    def give(k):
        def body(p):
            block = dot(place_t[span(p), :], grads[...])
            pack(block, msend.at[k, p], 0, groups, True)
            start(k, p, 0)

        each_partner(body)
        each_partner(lambda p: start(k, p, 1))
        pack(dot(place_t[span(me), :], grads[...]), mrecv.at[k, me], 0, groups, True)

    def take(k, part, first):
        lo, hi = ((0, some), (some, groups))[part]

        def body(p):
            finished(k, p, part)
            unpack(k, p, lo, hi, part == 0)

        unpack(k, me, lo, hi, part == 0)
        each_near(body)
        total = product(pick_t, first, rows, mine)
        each_far(body)
        return total + product(pick_t, first, rows, other)

    build_place_t(0)
    pl.semaphore_wait(barrier, n + 1)
    ask(0)

    for buf, ref in ((lbuf, left_ref), (rbuf, right_ref)):
        buf[...] = jnp.concatenate([ref[...], jnp.zeros((wide - width, rows), f32)], axis=0).T
    lcol[...] = jnp.broadcast_to(to_column(lstate_ref[...]), lcol.shape)
    rcol[...] = jnp.broadcast_to(to_column(rstate_ref[...]), rcol.shape)
    table[:rows, :] = lbuf[...].astype(bf16)
    table[rows:, :] = rbuf[...].astype(bf16)
    flat[...] = jnp.zeros(flat.shape, bf16)
    build_place_t(1)
    ask(1)

    rel_count = rel_raw.shape[1]

    def set_scale(s):
        column = to_column(kind_ref[s : s + 1, :].astype(f32)).astype(jnp.int32)
        chosen = one_hot(iota((edges, rel_count), 1) == column)
        last = ((1,), (1,))
        scale[s] = dot(chosen, rel_hi[...], last) + dot(chosen, rel_lo[...], last)

    for s in range(SUBS):
        if s == 0:
            ask_wait(0)
            build_pick(0)

            reply_all(0)

        if s == SUBS - 1:
            base_send[...] = rbuf[...].T[:width, :]
            onward(base_send, base_recv, 0).start()
        build_place(s)
        build_place_t(s)
        build_pick_t(s)
        if s == 0:
            rel_copy.wait()
            for ref in (rel_hi, rel_lo):
                ref[width:, :] = jnp.zeros((wide - width, rel_count), bf16)
            raw = rel_raw[...]
            upper = raw.astype(bf16)
            rel_hi[:width, :] = upper
            rel_lo[:width, :] = (raw - upper.astype(f32)).astype(bf16)
            set_scale(0)
            set_scale(1)
            ask_wait(1)
            build_pick(1)

        fetch(2 * s)
        factor = scale[s]
        source = fetched[:edges, :] * factor
        goal = fetched[edges : 2 * edges, :]
        others = fetched[2 * edges :, :]
        inv_q = lax.rsqrt(jnp.sum(source * source, axis=1, keepdims=True) + tiny)
        inv_t = lax.rsqrt(jnp.sum(goal * goal, axis=1, keepdims=True) + tiny)
        inv_n = lax.rsqrt(jnp.sum(others * others, axis=1, keepdims=True) + tiny)
        query = source * inv_q
        target = goal * inv_t
        noise = others * inv_n
        query_half = query.astype(bf16)
        noise_half = noise.astype(bf16)
        positive = sharp * jnp.sum(query * target, axis=1, keepdims=True)
        scores = sharp * dot(query_half, noise_half, ((1,), (1,)))
        raised = jnp.exp(positive)
        spread = jnp.exp(scores)
        total = raised + jnp.sum(spread, axis=1, keepdims=True)
        miss = raised / total - 1.0
        weights = (spread / total).astype(bf16)
        query_grad = sharp * (miss * target + dot(weights, noise_half))
        noise_grad = sharp * dot(weights, query_half, ((0,), (0,)))
        along_q = jnp.sum(query * query_grad, axis=1, keepdims=True)
        along_n = jnp.sum(noise * noise_grad, axis=1, keepdims=True)
        grads[:edges, :] = ((query_grad - query * along_q) * inv_q * factor).astype(bf16)
        grads[edges : 2 * edges, :] = (
            (sharp * miss * query - target * (miss * positive)) * inv_t
        ).astype(bf16)
        grads[2 * edges :, :] = ((noise_grad - noise * along_n) * inv_n).astype(bf16)

        give(2 * s + 1)
        for part, (buf, col, first) in enumerate(((lbuf, lcol, 0), (rbuf, rcol, rows))):
            grad = take(2 * s + 1, part, first)
            state = col[...][:, 0:1] + jnp.sum(grad * grad, axis=1, keepdims=True) * (1.0 / width)
            col[...] = jnp.broadcast_to(state, col.shape)
            step = rate * grad / (jnp.sqrt(state) + guard)
            if s + 1 == SUBS and first:
                step_send[...] = step.T[:width, :].astype(bf16)
                onward(step_send, step_recv, 1).start()
                hist_send[...] = jnp.broadcast_to(to_row(state), hist_send.shape)
                onward(hist_send, hist_recv, 2).start()
            else:
                new = buf[...] - step
                buf[...] = new
                if s + 1 < SUBS:
                    table[first : first + rows, :] = new.astype(bf16)
                    (reply_rest if part else reply_first)(2 * s + 2)

    lout_ref[...] = lbuf[...].T[:width, :]
    lsout_ref[...] = to_row(lcol[...][:, 0:1])
    for i, (source, goal) in enumerate(
        ((base_send, base_recv), (step_send, step_recv), (hist_send, hist_recv))
    ):
        onward(source, goal, i).wait()
    rout_ref[...] = base_recv[...] - step_recv[...].astype(f32)
    rsout_ref[...] = hist_recv[0:1, :]


def finish(*refs):
    for i in range(4):
        refs[4 + i][...] = refs[i][...]


def on_device(
    left_emb, right_emb, left_state, right_state, relations, src_rows, dst_rows, rel_ids, neg_rows
):
    rows, width = left_emb.shape
    rel_count = relations.shape[0]
    n = lax.axis_size("edge")
    nb = lax.axis_size("bucket")
    edges = src_rows.shape[2]
    cap = edges // n + 4
    slots = -(-3 * cap // PACK) * PACK
    wide = -(-width // LANE) * LANE
    chunks = wide // LANE - 1
    message = chunks * slots + PACK
    vmem = pl.BlockSpec(memory_space=pltpu.VMEM)
    shapes = (
        jax.ShapeDtypeStruct((width, rows), f32),
        jax.ShapeDtypeStruct((1, rows), f32),
    ) * 2
    out = pl.pallas_call(
        functools.partial(kernel, n, nb, width, cap, slots),
        out_shape=shapes,
        in_specs=[vmem] * 4 + [pl.BlockSpec(memory_space=pl.ANY)] + [vmem] * 4,
        out_specs=(vmem,) * 4,
        scratch_shapes=[
            pltpu.VMEM((rows, wide), f32),
            pltpu.VMEM((rows, wide), f32),
            pltpu.VMEM((rows, LANE), f32),
            pltpu.VMEM((rows, LANE), f32),
            pltpu.VMEM((2 * rows, wide), bf16),
            pltpu.VMEM((width, rel_count), f32),
            pltpu.VMEM((wide, rel_count), bf16),
            pltpu.VMEM((wide, rel_count), bf16),
            pltpu.VMEM((SUBS, edges, wide), f32),
            pltpu.VMEM((3 * edges, n * LANE), bf16),
            pltpu.VMEM((n * LANE, 3 * edges), bf16),
            pltpu.VMEM((n * LANE, 2 * rows), bf16),
            pltpu.VMEM((2 * rows, n * LANE), bf16),
            pltpu.VMEM((8, 3 * edges), f32),
            pltpu.VMEM((8, 3 * edges), f32),
            pltpu.VMEM((n * LANE, wide), bf16),
            pltpu.VMEM((3 * edges, wide), f32),
            pltpu.VMEM((3 * edges, wide), bf16),
            pltpu.VMEM((SUBS, n, 8, LANE), f32),
            pltpu.VMEM((SUBS, n, 8, LANE), f32),
            pltpu.VMEM((2 * SUBS, n, message, LANE), bf16),
            pltpu.VMEM((2 * SUBS, n, message, LANE), bf16),
            pltpu.VMEM((width, rows), f32),
            pltpu.VMEM((width, rows), f32),
            pltpu.VMEM((width, rows), bf16),
            pltpu.VMEM((width, rows), bf16),
            pltpu.VMEM((8, rows), f32),
            pltpu.VMEM((8, rows), f32),
            pltpu.SemaphoreType.DMA((SUBS, n)),
            pltpu.SemaphoreType.DMA((SUBS, n)),
            pltpu.SemaphoreType.DMA((2 * SUBS, 2, n)),
            pltpu.SemaphoreType.DMA((2 * SUBS, 2, n)),
            pltpu.SemaphoreType.DMA((2, 3)),
            pltpu.SemaphoreType.DMA,
        ],
        compiler_params=pltpu.CompilerParams(
            collective_id=0, has_side_effects=True, vmem_limit_bytes=56 * 1024 * 1024
        ),
    )(
        left_emb.T, right_emb.T, left_state.reshape(1, rows), right_state.reshape(1, rows),
        relations.T, src_rows[0], dst_rows[0], rel_ids[0], neg_rows[0],
    )
    out = pl.pallas_call(
        finish, out_shape=shapes, in_specs=[vmem] * 4, out_specs=(vmem,) * 4
    )(*out)
    return out[0].T, out[1].reshape(rows), out[2].T, out[3].reshape(rows)


def solution(mesh):
    return jax.shard_map(
        on_device,
        mesh=mesh,
        in_specs=(
            P(("bucket", "edge"), None),
            P(("bucket", "edge"), None),
            P(("bucket", "edge")),
            P(("bucket", "edge")),
            P(),
            P("bucket", None, "edge"),
            P("bucket", None, "edge"),
            P("bucket", None, "edge"),
            P("bucket", None, "edge"),
        ),
        out_specs=(
            P(("bucket", "edge"), None),
            P(("bucket", "edge")),
            P(("bucket", "edge"), None),
            P(("bucket", "edge")),
        ),
        check_vma=False,
    )
```

```python
import functools

import jax
import jax.numpy as jnp
from jax import lax
from jax.experimental import pallas as pl
from jax.experimental.pallas import tpu as pltpu
from jax.sharding import PartitionSpec as P

SUBS = 2
LANE = 128
PACK = 16

sharp = 40.0
rate = 0.5
tiny = 1e-06
guard = 1e-10

f32 = jnp.float32
bf16 = jnp.bfloat16
MESH = pl.DeviceIdType.MESH


def dot(first, second, dims=((1,), (0,))):
    return lax.dot_general(first, second, (dims, ((), ())), preferred_element_type=f32)


def iota(shape, dim):
    return lax.broadcasted_iota(jnp.int32, shape, dim)


def to_column(row):
    n = row.shape[1]
    same = iota((n, n), 0) == iota((n, n), 1)
    return jnp.sum(jnp.where(same, row, 0.0), axis=1, keepdims=True)


def to_row(column):
    n = column.shape[0]
    same = iota((n, n), 0) == iota((n, n), 1)
    return jnp.sum(jnp.where(same, column, 0.0), axis=0, keepdims=True)


def one_hot(where):
    return jnp.where(where, 1.0, 0.0).astype(bf16)


def kernel(
    n, nb, width, cap, slots,
    left_ref, right_ref, lstate_ref, rstate_ref, rel_hbm, src_ref, dst_ref, kind_ref, neg_ref,
    lout_ref, lsout_ref, rout_ref, rsout_ref,
    lbuf, rbuf, lcol, rcol, table, rel_raw, rel_hi, rel_lo, scale,
    place, place_t, pick, pick_t, prow, lrow, flat, fetched, grads, totals,
    wsend, wrecv, msend, mrecv, base_send, base_recv, step_send, step_recv, hist_send, hist_recv,
    wsem_s, wsem_r, msem_s, msem_r, ssem, rel_sem,
):
    rows = left_ref.shape[1]
    edges = src_ref.shape[1]
    wide = lbuf.shape[1]
    main = wide - LANE
    tail = width - main
    groups = slots // PACK
    chunks = main // LANE
    me = lax.axis_index("edge")
    mb = lax.axis_index("bucket")
    after = lax.rem(mb + 1, nb)
    before = lax.rem(mb + nb - 1, nb)

    half = n // 2
    mine = (me // half) * half
    other = half - mine

    def far(j):
        return other + lax.rem(me + j, half)

    def near(j):
        return mine + lax.rem(me + j, half)

    def each_far(body):
        def step(j, carry):
            body(far(j))
            return carry
        lax.fori_loop(0, half, step, 0)

    def each_near(body):
        def step(j, carry):
            body(near(j))
            return carry
        lax.fori_loop(1, half, step, 0)

    def each_partner(body):
        def step(j, carry):
            turn = n // 2 + ((j + 1) // 2) * (2 * (j % 2) - 1)
            body(lax.rem(me + turn + n, n))
            return carry
        lax.fori_loop(0, n - 1, step, 0)

    def each_index(body):
        def step(j, carry):
            body(j)
            return carry
        lax.fori_loop(0, n, step, 0)

    barrier = pltpu.get_barrier_semaphore()

    def greet(p):
        pl.semaphore_signal(barrier, inc=1, device_id=(mb, p), device_id_type=MESH)

    each_partner(greet)
    pl.semaphore_signal(barrier, inc=1, device_id=(after, me), device_id_type=MESH)
    pl.semaphore_signal(barrier, inc=1, device_id=(before, me), device_id_type=MESH)

    rel_copy = pltpu.make_async_copy(rel_hbm, rel_raw, rel_sem)
    rel_copy.start()

    def onward(source, goal, i):
        return pltpu.make_async_remote_copy(
            src_ref=source, dst_ref=goal, send_sem=ssem.at[0, i], recv_sem=ssem.at[1, i],
            device_id=(after, me), device_id_type=MESH,
        )

    def span(p):
        return pl.ds(pl.multiple_of(p * LANE, LANE), LANE)

    earlier = one_hot(iota((edges, edges), 0) < iota((edges, edges), 1))
    holder = iota((n, edges), 0)

    def find(s):
        for t, ids_ref in enumerate((src_ref, dst_ref, neg_ref)):
            ids = ids_ref[s : s + 1, :]
            inside = (ids >= holder * rows) & (ids < holder * rows + rows)
            hits = jnp.where(inside, 1.0, 0.0)
            rank = dot(hits.astype(bf16), earlier)
            at = jnp.sum(
                hits * ((holder * LANE + t * cap).astype(f32) + rank), axis=0, keepdims=True
            )
            owner = jnp.sum(hits * holder.astype(f32), axis=0, keepdims=True)
            prow[s : s + 1, t * edges : (t + 1) * edges] = at
            lrow[s : s + 1, t * edges : (t + 1) * edges] = ids.astype(f32) - owner * rows

    def build_place_t(s):
        row = prow[s : s + 1, :].astype(jnp.int32)

        def body(p):
            place_t[span(p), :] = one_hot(iota((LANE, 3 * edges), 0) + p * LANE == row)

        each_index(body)

    def build_place(s):
        for t in range(3):
            column = to_column(prow[s : s + 1, t * edges : (t + 1) * edges]).astype(jnp.int32)

            def body(p):
                place[t * edges : (t + 1) * edges, span(p)] = one_hot(
                    iota((edges, LANE), 1) + p * LANE == column
                )

            each_index(body)

    def prepare(s):
        local = lrow[s : s + 1, :]
        upper = iota((8, 3 * edges), 0)
        lhs = jnp.where(upper == 0, local, jnp.where(upper == 1, 1.0, 0.0)).astype(bf16)
        lane = iota((1, LANE), 1)
        offset = jnp.where(lane < cap, 0.0, float(rows))

        found = dot(lhs, place_t[...], ((1,), (1,)))
        for p in range(n):
            part = found[:, p * LANE : (p + 1) * LANE]
            row = jnp.where(part[1:2] > 0.5, part[0:1] + offset, -1.0)
            wsend[s, p] = jnp.broadcast_to(row, (8, LANE))

    def ask(s):
        each_partner(lambda p: ask_copy(s, p).start())
        wrecv[s, me] = wsend[s, me]

    def ask_copy(s, p):
        return pltpu.make_async_remote_copy(
            src_ref=wsend.at[s, p], dst_ref=wrecv.at[s, me],
            send_sem=wsem_s.at[s, p], recv_sem=wsem_r.at[s, me],
            device_id=(mb, p), device_id_type=MESH,
        )

    def ask_wait(s):
        def body(p):
            copy = pltpu.make_async_remote_copy(
                src_ref=wsend.at[s, p], dst_ref=wrecv.at[s, p],
                send_sem=wsem_s.at[s, p], recv_sem=wsem_r.at[s, p],
                device_id=(mb, p), device_id_type=MESH,
            )
            copy.wait()

        each_partner(body)

    def build_pick(s, p):
        column = to_column(wrecv[s, p][0:1, :]).astype(jnp.int32)
        pick[span(p), :] = one_hot(iota((LANE, 2 * rows), 1) == column)

    def build_pick_t(s):
        def body(p):
            row = wrecv[s, p][0:1, :].astype(jnp.int32)
            pick_t[:, span(p)] = one_hot(iota((2 * rows, LANE), 0) == row)

        each_index(body)

    def pack(block, ref):
        for c in range(chunks):
            ref[c * slots : (c + 1) * slots, :] = block[:slots, c * LANE : (c + 1) * LANE].astype(bf16)
        ends = block[:, main:]
        total = ends[:PACK]
        for g in range(1, groups):
            total = total + pltpu.roll(ends[g * PACK : (g + 1) * PACK], g * tail, 1)
        ref[chunks * slots :, :] = total.astype(bf16)

    def piece(k, p, slot):
        return pltpu.make_async_remote_copy(
            src_ref=msend.at[k, p], dst_ref=mrecv.at[k, slot],
            send_sem=msem_s.at[k, p], recv_sem=msem_r.at[k, slot],
            device_id=(mb, p), device_id_type=MESH,
        )

    keep = iota((PACK, LANE), 1) < tail

    def unpack(k, p):
        at = pl.multiple_of(p * LANE, LANE)
        for c in range(chunks):
            flat[pl.ds(at, slots), c * LANE : (c + 1) * LANE] = mrecv[
                k, p, c * slots : (c + 1) * slots, :
            ]
        ends = mrecv[k, p, chunks * slots : chunks * slots + PACK, :].astype(f32)
        for g in range(groups):
            part = ends if g == 0 else pltpu.roll(ends, LANE - g * tail, 1)
            flat[pl.ds(at + g * PACK, PACK), main:] = jnp.where(keep, part, 0.0).astype(bf16)

    def arrive(k):
        def body(p):
            piece(k, p, p).wait()
            unpack(k, p)

        return body

    def exchange(k, make):
        def body(p):
            pack(make(p), msend.at[k, p])
            piece(k, p, me).start()

        each_partner(body)
        pack(make(me), mrecv.at[k, me])

    def half_span(first):
        return pl.ds(pl.multiple_of(first * LANE, LANE * half), LANE * half)

    def product(lhs_ref, first, count, start_at):
        lines = half_span(start_at)
        return dot(lhs_ref[first : first + count, lines], flat[lines, :])

    def fetch(k):
        unpack(k, me)
        each_near(arrive(k))
        for t in range(3):
            fetched[t * edges : (t + 1) * edges, :] = product(place, t * edges, edges, mine)
        each_far(arrive(k))
        for t in range(3):
            fetched[t * edges : (t + 1) * edges, :] += product(place, t * edges, edges, other)

    def take(k):
        unpack(k, me)
        each_near(arrive(k))
        for first in (rows, 0):
            totals[first : first + rows, :] = product(pick_t, first, rows, mine)
        each_far(arrive(k))

    find(0)
    build_place_t(0)
    prepare(0)
    pl.semaphore_wait(barrier, n + 1)
    ask(0)

    for buf, ref, first in ((lbuf, left_ref, 0), (rbuf, right_ref, rows)):
        turned = jnp.concatenate([ref[...], jnp.zeros((wide - width, rows), f32)], axis=0).T
        buf[...] = turned
        table[first : first + rows, :] = turned.astype(bf16)

    rel_count = rel_raw.shape[1]

    def set_scale(s):
        column = to_column(kind_ref[s : s + 1, :].astype(f32)).astype(jnp.int32)
        chosen = one_hot(iota((edges, rel_count), 1) == column)
        last = ((1,), (1,))
        scale[s] = dot(chosen, rel_hi[...], last) + dot(chosen, rel_lo[...], last)

    for s in range(SUBS):
        def reply(p):
            if s == 0:
                build_pick(0, p)
            return dot(pick[span(p), :], table[...])

        if s == 0:
            ask_wait(0)
        exchange(2 * s, reply)

        if s == SUBS - 1:
            base_send[...] = rbuf[...].T[:width, :]
            onward(base_send, base_recv, 0).start()
        if s == 0:
            find(1)
            build_place_t(1)
            prepare(1)
            ask(1)
            lcol[...] = jnp.broadcast_to(to_column(lstate_ref[...]), lcol.shape)
            rcol[...] = jnp.broadcast_to(to_column(rstate_ref[...]), rcol.shape)
            flat[...] = jnp.zeros(flat.shape, bf16)
        build_place(s)
        build_place_t(s)
        build_pick_t(s)
        if s == 0:
            rel_copy.wait()
            for ref in (rel_hi, rel_lo):
                ref[width:, :] = jnp.zeros((wide - width, rel_count), bf16)
            raw = rel_raw[...]
            upper = raw.astype(bf16)
            rel_hi[:width, :] = upper
            rel_lo[:width, :] = (raw - upper.astype(f32)).astype(bf16)
            set_scale(0)
            set_scale(1)
            ask_wait(1)
            each_index(lambda p: build_pick(1, p))

        fetch(2 * s)
        factor = scale[s]
        source = fetched[:edges, :] * factor
        goal = fetched[edges : 2 * edges, :]
        others = fetched[2 * edges :, :]
        inv_q = lax.rsqrt(jnp.sum(source * source, axis=1, keepdims=True) + tiny)
        inv_t = lax.rsqrt(jnp.sum(goal * goal, axis=1, keepdims=True) + tiny)
        inv_n = lax.rsqrt(jnp.sum(others * others, axis=1, keepdims=True) + tiny)
        query = source * inv_q
        target = goal * inv_t
        noise = others * inv_n
        query_half = query.astype(bf16)
        noise_half = noise.astype(bf16)
        positive = sharp * jnp.sum(query * target, axis=1, keepdims=True)
        scores = sharp * dot(query_half, noise_half, ((1,), (1,)))
        raised = jnp.exp(positive)
        spread = jnp.exp(scores)
        total = raised + jnp.sum(spread, axis=1, keepdims=True)
        miss = raised / total - 1.0
        weights = (spread / total).astype(bf16)
        query_grad = sharp * (miss * target + dot(weights, noise_half))
        noise_grad = sharp * dot(weights, query_half, ((0,), (0,)))
        along_q = jnp.sum(query * query_grad, axis=1, keepdims=True)
        along_n = jnp.sum(noise * noise_grad, axis=1, keepdims=True)
        grads[:edges, :] = ((query_grad - query * along_q) * inv_q * factor).astype(bf16)
        grads[edges : 2 * edges, :] = (
            (sharp * miss * query - target * (miss * positive)) * inv_t
        ).astype(bf16)
        grads[2 * edges :, :] = ((noise_grad - noise * along_n) * inv_n).astype(bf16)

        exchange(2 * s + 1, lambda p: dot(place_t[span(p), :], grads[...]))
        take(2 * s + 1)
        for buf, col, first in ((rbuf, rcol, rows), (lbuf, lcol, 0)):
            grad = totals[first : first + rows, :] + product(pick_t, first, rows, other)
            state = col[...][:, 0:1] + jnp.sum(grad * grad, axis=1, keepdims=True) * (1.0 / width)
            col[...] = jnp.broadcast_to(state, col.shape)
            step = rate * grad / (jnp.sqrt(state) + guard)
            if s + 1 == SUBS and first:
                step_send[...] = step.T[:width, :].astype(bf16)
                onward(step_send, step_recv, 1).start()
                hist_send[...] = jnp.broadcast_to(to_row(state), hist_send.shape)
                onward(hist_send, hist_recv, 2).start()
            else:
                new = buf[...] - step
                buf[...] = new
                if s + 1 < SUBS:
                    table[first : first + rows, :] = new.astype(bf16)

    lout_ref[...] = lbuf[...].T[:width, :]
    lsout_ref[...] = to_row(lcol[...][:, 0:1])
    for i, (source, goal) in enumerate(
        ((base_send, base_recv), (step_send, step_recv), (hist_send, hist_recv))
    ):
        onward(source, goal, i).wait()
    rout_ref[...] = base_recv[...] - step_recv[...].astype(f32)
    rsout_ref[...] = hist_recv[0:1, :]


def finish(*refs):
    for i in range(4):
        refs[4 + i][...] = refs[i][...]


def on_device(
    left_emb, right_emb, left_state, right_state, relations, src_rows, dst_rows, rel_ids, neg_rows
):
    rows, width = left_emb.shape
    rel_count = relations.shape[0]
    n = lax.axis_size("edge")
    nb = lax.axis_size("bucket")
    edges = src_rows.shape[2]
    cap = edges // n + 4
    slots = -(-3 * cap // PACK) * PACK
    wide = -(-width // LANE) * LANE
    chunks = wide // LANE - 1
    message = chunks * slots + PACK
    vmem = pl.BlockSpec(memory_space=pltpu.VMEM)
    shapes = (
        jax.ShapeDtypeStruct((width, rows), f32),
        jax.ShapeDtypeStruct((1, rows), f32),
    ) * 2
    out = pl.pallas_call(
        functools.partial(kernel, n, nb, width, cap, slots),
        out_shape=shapes,
        in_specs=[vmem] * 4 + [pl.BlockSpec(memory_space=pl.ANY)] + [vmem] * 4,
        out_specs=(vmem,) * 4,
        scratch_shapes=[
            pltpu.VMEM((rows, wide), f32),
            pltpu.VMEM((rows, wide), f32),
            pltpu.VMEM((rows, LANE), f32),
            pltpu.VMEM((rows, LANE), f32),
            pltpu.VMEM((2 * rows, wide), bf16),
            pltpu.VMEM((width, rel_count), f32),
            pltpu.VMEM((wide, rel_count), bf16),
            pltpu.VMEM((wide, rel_count), bf16),
            pltpu.VMEM((SUBS, edges, wide), f32),
            pltpu.VMEM((3 * edges, n * LANE), bf16),
            pltpu.VMEM((n * LANE, 3 * edges), bf16),
            pltpu.VMEM((n * LANE, 2 * rows), bf16),
            pltpu.VMEM((2 * rows, n * LANE), bf16),
            pltpu.VMEM((8, 3 * edges), f32),
            pltpu.VMEM((8, 3 * edges), f32),
            pltpu.VMEM((n * LANE, wide), bf16),
            pltpu.VMEM((3 * edges, wide), f32),
            pltpu.VMEM((3 * edges, wide), bf16),
            pltpu.VMEM((2 * rows, wide), f32),
            pltpu.VMEM((SUBS, n, 8, LANE), f32),
            pltpu.VMEM((SUBS, n, 8, LANE), f32),
            pltpu.VMEM((2 * SUBS, n, message, LANE), bf16),
            pltpu.VMEM((2 * SUBS, n, message, LANE), bf16),
            pltpu.VMEM((width, rows), f32),
            pltpu.VMEM((width, rows), f32),
            pltpu.VMEM((width, rows), bf16),
            pltpu.VMEM((width, rows), bf16),
            pltpu.VMEM((8, rows), f32),
            pltpu.VMEM((8, rows), f32),
            pltpu.SemaphoreType.DMA((SUBS, n)),
            pltpu.SemaphoreType.DMA((SUBS, n)),
            pltpu.SemaphoreType.DMA((2 * SUBS, n)),
            pltpu.SemaphoreType.DMA((2 * SUBS, n)),
            pltpu.SemaphoreType.DMA((2, 3)),
            pltpu.SemaphoreType.DMA,
        ],
        compiler_params=pltpu.CompilerParams(
            collective_id=0, has_side_effects=True, vmem_limit_bytes=56 * 1024 * 1024
        ),
    )(
        left_emb.T, right_emb.T, left_state.reshape(1, rows), right_state.reshape(1, rows),
        relations.T, src_rows[0], dst_rows[0], rel_ids[0], neg_rows[0],
    )
    out = pl.pallas_call(
        finish, out_shape=shapes, in_specs=[vmem] * 4, out_specs=(vmem,) * 4
    )(*out)
    return out[0].T, out[1].reshape(rows), out[2].T, out[3].reshape(rows)


def solution(mesh):
    return jax.shard_map(
        on_device,
        mesh=mesh,
        in_specs=(
            P(("bucket", "edge"), None),
            P(("bucket", "edge"), None),
            P(("bucket", "edge")),
            P(("bucket", "edge")),
            P(),
            P("bucket", None, "edge"),
            P("bucket", None, "edge"),
            P("bucket", None, "edge"),
            P("bucket", None, "edge"),
        ),
        out_specs=(
            P(("bucket", "edge"), None),
            P(("bucket", "edge")),
            P(("bucket", "edge"), None),
            P(("bucket", "edge")),
        ),
        check_vma=False,
    )
```

```python
import functools

import jax
import jax.numpy as jnp
from jax import lax
from jax.experimental import pallas as pl
from jax.experimental.pallas import tpu as pltpu
from jax.sharding import PartitionSpec as P

SUBS = 2
LANE = 128
PACK = 16

sharp = 40.0
rate = 0.5
tiny = 1e-06
guard = 1e-10

f32 = jnp.float32
bf16 = jnp.bfloat16
MESH = pl.DeviceIdType.MESH


def dot(first, second, dims=((1,), (0,))):
    return lax.dot_general(first, second, (dims, ((), ())), preferred_element_type=f32)


def iota(shape, dim):
    return lax.broadcasted_iota(jnp.int32, shape, dim)


def to_column(row):
    n = row.shape[1]
    same = iota((n, n), 0) == iota((n, n), 1)
    return jnp.sum(jnp.where(same, row, 0.0), axis=1, keepdims=True)


def to_row(column):
    n = column.shape[0]
    same = iota((n, n), 0) == iota((n, n), 1)
    return jnp.sum(jnp.where(same, column, 0.0), axis=0, keepdims=True)


def one_hot(where):
    return jnp.where(where, 1.0, 0.0).astype(bf16)


def kernel(
    n, nb, width, cap, slots,
    left_ref, right_ref, lstate_ref, rstate_ref, rel_hbm, src_ref, dst_ref, kind_ref, neg_ref,
    lout_ref, lsout_ref, rout_ref, rsout_ref,
    lbuf, rbuf, lcol, rcol, table, rel_raw, rel_hi, rel_lo, scale,
    place, place_t, pick, pick_t, prow, lrow, flat, fetched, grads,
    wsend, wrecv, msend, mrecv, base_send, base_recv, step_send, step_recv, hist_send, hist_recv,
    wsem_s, wsem_r, msem_s, msem_r, ssem, rel_sem,
):
    rows = left_ref.shape[1]
    edges = src_ref.shape[1]
    wide = lbuf.shape[1]
    main = wide - LANE
    tail = width - main
    groups = slots // PACK
    chunks = main // LANE
    me = lax.axis_index("edge")
    mb = lax.axis_index("bucket")
    after = lax.rem(mb + 1, nb)
    before = lax.rem(mb + nb - 1, nb)

    def each_partner(body):
        def step(j, carry):
            turn = n // 2 + ((j + 1) // 2) * (2 * (j % 2) - 1)
            body(lax.rem(me + turn + n, n))
            return carry
        lax.fori_loop(0, n - 1, step, 0)

    def each_index(body):
        def step(j, carry):
            body(j)
            return carry
        lax.fori_loop(0, n, step, 0, unroll=n <= 8)

    barrier = pltpu.get_barrier_semaphore()

    def greet(p):
        pl.semaphore_signal(barrier, inc=1, device_id=(mb, p), device_id_type=MESH)

    each_partner(greet)
    pl.semaphore_signal(barrier, inc=1, device_id=(after, me), device_id_type=MESH)
    pl.semaphore_signal(barrier, inc=1, device_id=(before, me), device_id_type=MESH)

    rel_copy = pltpu.make_async_copy(rel_hbm, rel_raw, rel_sem)
    rel_copy.start()

    def onward(source, goal, i):
        return pltpu.make_async_remote_copy(
            src_ref=source, dst_ref=goal, send_sem=ssem.at[0, i], recv_sem=ssem.at[1, i],
            device_id=(after, me), device_id_type=MESH,
        )

    def span(p):
        return pl.ds(pl.multiple_of(p * LANE, LANE), LANE)

    earlier = one_hot(iota((edges, edges), 0) < iota((edges, edges), 1))
    holder = iota((n, edges), 0)

    def find(s):
        for t, ids_ref in enumerate((src_ref, dst_ref, neg_ref)):
            ids = ids_ref[s : s + 1, :]
            inside = (ids >= holder * rows) & (ids < holder * rows + rows)
            hits = jnp.where(inside, 1.0, 0.0)
            rank = dot(hits.astype(bf16), earlier)
            at = jnp.sum(
                hits * ((holder * LANE + t * cap).astype(f32) + rank), axis=0, keepdims=True
            )
            owner = jnp.sum(hits * holder.astype(f32), axis=0, keepdims=True)
            prow[s : s + 1, t * edges : (t + 1) * edges] = at
            lrow[s : s + 1, t * edges : (t + 1) * edges] = ids.astype(f32) - owner * rows

    def build_place_t(s):
        row = prow[s : s + 1, :].astype(jnp.int32)

        def body(p):
            place_t[s, span(p), :] = one_hot(iota((LANE, 3 * edges), 0) + p * LANE == row)

        each_index(body)

    def build_place(s):
        for t in range(3):
            column = to_column(prow[s : s + 1, t * edges : (t + 1) * edges]).astype(jnp.int32)

            def body(p):
                place[t * edges : (t + 1) * edges, span(p)] = one_hot(
                    iota((edges, LANE), 1) + p * LANE == column
                )

            each_index(body)

    def prepare(s):
        local = lrow[s : s + 1, :]
        upper = iota((8, 3 * edges), 0)
        lhs = jnp.where(upper == 0, local, jnp.where(upper == 1, 1.0, 0.0)).astype(bf16)
        lane = iota((1, LANE), 1)
        offset = jnp.where(lane < cap, 0.0, float(rows))

        found = dot(lhs, place_t[s], ((1,), (1,)))
        for p in range(n):
            part = found[:, p * LANE : (p + 1) * LANE]
            row = jnp.where(part[1:2] > 0.5, part[0:1] + offset, -1.0)
            wsend[s, p] = jnp.broadcast_to(row, (8, LANE))

    def ask(s):
        each_partner(lambda p: ask_copy(s, p).start())
        wrecv[s, me] = wsend[s, me]

    def ask_copy(s, p):
        return pltpu.make_async_remote_copy(
            src_ref=wsend.at[s, p], dst_ref=wrecv.at[s, me],
            send_sem=wsem_s.at[s, p], recv_sem=wsem_r.at[s, me],
            device_id=(mb, p), device_id_type=MESH,
        )

    def ask_wait(s):
        def body(p):
            copy = pltpu.make_async_remote_copy(
                src_ref=wsend.at[s, p], dst_ref=wrecv.at[s, p],
                send_sem=wsem_s.at[s, p], recv_sem=wsem_r.at[s, p],
                device_id=(mb, p), device_id_type=MESH,
            )
            copy.wait()

        each_partner(body)

    def build_pick(s, p):
        column = to_column(wrecv[s, p][0:1, :]).astype(jnp.int32)
        pick[span(p), :] = one_hot(iota((LANE, 2 * rows), 1) == column)

    def build_pick_t(s):
        def body(p):
            row = wrecv[s, p][0:1, :].astype(jnp.int32)
            pick_t[:, span(p)] = one_hot(iota((2 * rows, LANE), 0) == row)

        each_index(body)

    def pack(block, ref):
        for c in range(chunks):
            ref[c * slots : (c + 1) * slots, :] = block[:slots, c * LANE : (c + 1) * LANE].astype(bf16)
        ends = block[:, main:]
        total = ends[:PACK]
        for g in range(1, groups):
            total = total + pltpu.roll(ends[g * PACK : (g + 1) * PACK], g * tail, 1)
        ref[chunks * slots :, :] = total.astype(bf16)

    def piece(k, p, slot):
        return pltpu.make_async_remote_copy(
            src_ref=msend.at[k, p], dst_ref=mrecv.at[k, slot],
            send_sem=msem_s.at[k, p], recv_sem=msem_r.at[k, slot],
            device_id=(mb, p), device_id_type=MESH,
        )

    keep = iota((PACK, LANE), 1) < tail

    def unpack(k, p):
        at = pl.multiple_of(p * LANE, LANE)
        for c in range(chunks):
            flat[pl.ds(at, slots), c * LANE : (c + 1) * LANE] = mrecv[
                k, p, c * slots : (c + 1) * slots, :
            ]
        ends = mrecv[k, p, chunks * slots : chunks * slots + PACK, :].astype(f32)
        for g in range(groups):
            part = ends if g == 0 else pltpu.roll(ends, LANE - g * tail, 1)
            flat[pl.ds(at + g * PACK, PACK), main:] = jnp.where(keep, part, 0.0).astype(bf16)

    def arrive(k):
        def body(p):
            piece(k, p, p).wait()
            unpack(k, p)

        return body

    def exchange(k, make):
        def body(p):
            pack(make(p), msend.at[k, p])
            piece(k, p, me).start()

        each_partner(body)
        pack(make(me), mrecv.at[k, me])

    def product(lhs_ref, first, count):
        depth = n * LANE
        step = min(depth, 1024)
        total = None
        for k in range(0, depth, step):
            part = dot(lhs_ref[first : first + count, k : k + step], flat[k : k + step, :])
            total = part if total is None else total + part
        return total

    def collect(k):
        unpack(k, me)
        each_partner(arrive(k))

    find(0)
    build_place_t(0)
    prepare(0)
    pl.semaphore_wait(barrier, n + 1)
    ask(0)

    for buf, ref, first in ((lbuf, left_ref, 0), (rbuf, right_ref, rows)):
        turned = jnp.concatenate([ref[...], jnp.zeros((wide - width, rows), f32)], axis=0).T
        buf[...] = turned
        table[first : first + rows, :] = turned.astype(bf16)

    rel_count = rel_raw.shape[1]

    def set_scale(s):
        column = to_column(kind_ref[s : s + 1, :].astype(f32)).astype(jnp.int32)
        chosen = one_hot(iota((edges, rel_count), 1) == column)
        last = ((1,), (1,))
        scale[s] = dot(chosen, rel_hi[...], last) + dot(chosen, rel_lo[...], last)

    for s in range(SUBS):
        def reply(p):
            if s == 0:
                build_pick(0, p)
            return dot(pick[span(p), :], table[...])

        if s == 0:
            ask_wait(0)
        exchange(2 * s, reply)

        if s == SUBS - 1:
            base_send[...] = rbuf[...].T[:width, :]
            onward(base_send, base_recv, 0).start()
        if s == 0:
            find(1)
            build_place_t(1)
            prepare(1)
            ask(1)
            lcol[...] = jnp.broadcast_to(to_column(lstate_ref[...]), lcol.shape)
            rcol[...] = jnp.broadcast_to(to_column(rstate_ref[...]), rcol.shape)
            flat[...] = jnp.zeros(flat.shape, bf16)
        if s == 0:
            build_place(0)
        build_pick_t(s)
        if s == 0:
            rel_copy.wait()
            for ref in (rel_hi, rel_lo):
                ref[width:, :] = jnp.zeros((wide - width, rel_count), bf16)
            raw = rel_raw[...]
            upper = raw.astype(bf16)
            rel_hi[:width, :] = upper
            rel_lo[:width, :] = (raw - upper.astype(f32)).astype(bf16)
            set_scale(0)

        collect(2 * s)
        for t in range(3):
            fetched[t * edges : (t + 1) * edges, :] = product(place, t * edges, edges)

        factor = scale[s]
        source = fetched[:edges, :] * factor
        goal = fetched[edges : 2 * edges, :]
        others = fetched[2 * edges :, :]
        inv_q = lax.rsqrt(jnp.sum(source * source, axis=1, keepdims=True) + tiny)
        inv_t = lax.rsqrt(jnp.sum(goal * goal, axis=1, keepdims=True) + tiny)
        inv_n = lax.rsqrt(jnp.sum(others * others, axis=1, keepdims=True) + tiny)
        query = source * inv_q
        target = goal * inv_t
        noise = others * inv_n
        query_half = query.astype(bf16)
        noise_half = noise.astype(bf16)
        positive = sharp * jnp.sum(query * target, axis=1, keepdims=True)
        scores = sharp * dot(query_half, noise_half, ((1,), (1,)))
        raised = jnp.exp(positive)
        spread = jnp.exp(scores)
        total = raised + jnp.sum(spread, axis=1, keepdims=True)
        miss = raised / total - 1.0
        weights = (spread / total).astype(bf16)
        query_grad = sharp * (miss * target + dot(weights, noise_half))
        noise_grad = sharp * dot(weights, query_half, ((0,), (0,)))
        along_q = jnp.sum(query * query_grad, axis=1, keepdims=True)
        along_n = jnp.sum(noise * noise_grad, axis=1, keepdims=True)
        grads[:edges, :] = ((query_grad - query * along_q) * inv_q * factor).astype(bf16)
        grads[edges : 2 * edges, :] = (
            (sharp * miss * query - target * (miss * positive)) * inv_t
        ).astype(bf16)
        grads[2 * edges :, :] = ((noise_grad - noise * along_n) * inv_n).astype(bf16)

        exchange(2 * s + 1, lambda p: dot(place_t[s, span(p), :], grads[...]))
        if s + 1 < SUBS:
            ask_wait(s + 1)
            each_index(lambda p: build_pick(s + 1, p))
            build_place(s + 1)
            set_scale(s + 1)
        collect(2 * s + 1)
        for buf, col, first in ((rbuf, rcol, rows), (lbuf, lcol, 0)):
            grad = product(pick_t, first, rows)
            state = col[...][:, 0:1] + jnp.sum(grad * grad, axis=1, keepdims=True) * (1.0 / width)
            col[...] = jnp.broadcast_to(state, col.shape)
            step = rate * grad / (jnp.sqrt(state) + guard)
            if s + 1 == SUBS and first:
                step_send[...] = step.T[:width, :].astype(bf16)
                onward(step_send, step_recv, 1).start()
                hist_send[...] = jnp.broadcast_to(to_row(state), hist_send.shape)
                onward(hist_send, hist_recv, 2).start()
            else:
                new = buf[...] - step
                buf[...] = new
                if s + 1 < SUBS:
                    table[first : first + rows, :] = new.astype(bf16)

    lout_ref[...] = lbuf[...].T[:width, :]
    lsout_ref[...] = to_row(lcol[...][:, 0:1])
    for i, (source, goal) in enumerate(
        ((base_send, base_recv), (step_send, step_recv), (hist_send, hist_recv))
    ):
        onward(source, goal, i).wait()
    rout_ref[...] = base_recv[...] - step_recv[...].astype(f32)
    rsout_ref[...] = hist_recv[0:1, :]


def finish(*refs):
    for i in range(4):
        refs[4 + i][...] = refs[i][...]


def on_device(
    left_emb, right_emb, left_state, right_state, relations, src_rows, dst_rows, rel_ids, neg_rows
):
    rows, width = left_emb.shape
    rel_count = relations.shape[0]
    n = lax.axis_size("edge")
    nb = lax.axis_size("bucket")
    edges = src_rows.shape[2]
    cap = edges // n + 4
    slots = -(-3 * cap // PACK) * PACK
    wide = -(-width // LANE) * LANE
    chunks = wide // LANE - 1
    message = chunks * slots + PACK
    vmem = pl.BlockSpec(memory_space=pltpu.VMEM)
    shapes = (
        jax.ShapeDtypeStruct((width, rows), f32),
        jax.ShapeDtypeStruct((1, rows), f32),
    ) * 2
    out = pl.pallas_call(
        functools.partial(kernel, n, nb, width, cap, slots),
        out_shape=shapes,
        in_specs=[vmem] * 4 + [pl.BlockSpec(memory_space=pl.ANY)] + [vmem] * 4,
        out_specs=(vmem,) * 4,
        scratch_shapes=[
            pltpu.VMEM((rows, wide), f32),
            pltpu.VMEM((rows, wide), f32),
            pltpu.VMEM((rows, LANE), f32),
            pltpu.VMEM((rows, LANE), f32),
            pltpu.VMEM((2 * rows, wide), bf16),
            pltpu.VMEM((width, rel_count), f32),
            pltpu.VMEM((wide, rel_count), bf16),
            pltpu.VMEM((wide, rel_count), bf16),
            pltpu.VMEM((SUBS, edges, wide), f32),
            pltpu.VMEM((3 * edges, n * LANE), bf16),
            pltpu.VMEM((SUBS, n * LANE, 3 * edges), bf16),
            pltpu.VMEM((n * LANE, 2 * rows), bf16),
            pltpu.VMEM((2 * rows, n * LANE), bf16),
            pltpu.VMEM((8, 3 * edges), f32),
            pltpu.VMEM((8, 3 * edges), f32),
            pltpu.VMEM((n * LANE, wide), bf16),
            pltpu.VMEM((3 * edges, wide), f32),
            pltpu.VMEM((3 * edges, wide), bf16),
            pltpu.VMEM((SUBS, n, 8, LANE), f32),
            pltpu.VMEM((SUBS, n, 8, LANE), f32),
            pltpu.VMEM((2 * SUBS, n, message, LANE), bf16),
            pltpu.VMEM((2 * SUBS, n, message, LANE), bf16),
            pltpu.VMEM((width, rows), f32),
            pltpu.VMEM((width, rows), f32),
            pltpu.VMEM((width, rows), bf16),
            pltpu.VMEM((width, rows), bf16),
            pltpu.VMEM((8, rows), f32),
            pltpu.VMEM((8, rows), f32),
            pltpu.SemaphoreType.DMA((SUBS, n)),
            pltpu.SemaphoreType.DMA((SUBS, n)),
            pltpu.SemaphoreType.DMA((2 * SUBS, n)),
            pltpu.SemaphoreType.DMA((2 * SUBS, n)),
            pltpu.SemaphoreType.DMA((2, 3)),
            pltpu.SemaphoreType.DMA,
        ],
        compiler_params=pltpu.CompilerParams(
            collective_id=0, has_side_effects=True, vmem_limit_bytes=56 * 1024 * 1024
        ),
    )(
        left_emb.T, right_emb.T, left_state.reshape(1, rows), right_state.reshape(1, rows),
        relations.T, src_rows[0], dst_rows[0], rel_ids[0], neg_rows[0],
    )
    out = pl.pallas_call(
        finish, out_shape=shapes, in_specs=[vmem] * 4, out_specs=(vmem,) * 4
    )(*out)
    return out[0].T, out[1].reshape(rows), out[2].T, out[3].reshape(rows)


def solution(mesh):
    return jax.shard_map(
        on_device,
        mesh=mesh,
        in_specs=(
            P(("bucket", "edge"), None),
            P(("bucket", "edge"), None),
            P(("bucket", "edge")),
            P(("bucket", "edge")),
            P(),
            P("bucket", None, "edge"),
            P("bucket", None, "edge"),
            P("bucket", None, "edge"),
            P("bucket", None, "edge"),
        ),
        out_specs=(
            P(("bucket", "edge"), None),
            P(("bucket", "edge")),
            P(("bucket", "edge"), None),
            P(("bucket", "edge")),
        ),
        check_vma=False,
    )
```
